256 devices in a mesh: leaf: 8 (over z_lo, core), front: 32 (over x, y, z_hi).
Axes of the slice: x: 4, y: 4, z: 8 (z_hi: 2, z_lo: 4; z = z_hi * 4 + z_lo), core: 2. Of those that a mesh axis runs over, the one named last changes fastest.
Arguments:
- child_update: float32 [8, 3840, 3840], P('leaf', 'front'), as said below
- entries: float32 [3, 8, 4096, 4096], P(None, 'leaf', 'front'), as said below
- slots: int32 [3, 8, 4096], replicated, may hold values from -1 to 3839, as said below
Outputs:
- multipliers: float32 [8, 3, 3840, 256], P('leaf', None, 'front')
- top_schur: float32 [3840, 3840], P('front', 'leaf')
The draws below stay inside these ranges and needn't reach their ends.
Inputs may be any that keep to these rules, and one draw needn't show every extreme that they name: In every row slots[t, m, :] each of 0 .. 3839 appears exactly once and the other 256 entries are -1. Every matrix entries[t, m] is symmetric and positive definite. Every matrix child_update[m] is symmetric and positive definite.
All inputs are finite; a program needn't handle non-finite values.
Results may differ from the reference program's by a relative error of at most 0.00015.
Values sent between devices are 32-bit elements; how exact they have to be, the bound alone decides.
No kernel may reach another device: no remote copies, remote signals or barrier semaphores. Data moves between devices by JAX's collectives and lax.ppermute only.
A program may use at most 128 MiB of HBM per device.

```python
import jax
import jax.numpy as jnp
from jax import lax

ROWS = 128
F = 4096
U = 3840
PIVB = 8
LEAVES = 8
LEVELS = 3
N_FRONT = 32


point_dims = 4


kernel_reach = 0.5


def kernel_matrix(block_key, matrix_order, point_power, scale_low, scale_high, diagonal_low, diagonal_high):
    point_key, scale_key, diagonal_key = jax.random.split(block_key, 3)
    points = jax.random.uniform(point_key, (point_dims, matrix_order), jnp.float32) ** point_power
    scales = jax.random.uniform(scale_key, (matrix_order,), jnp.float32, scale_low, scale_high)
    distance = jnp.zeros((matrix_order, matrix_order), jnp.float32)
    for dim_index in range(point_dims):
        distance = distance + jnp.abs(points[dim_index][:, None] - points[dim_index][None, :])
    kernel = jnp.exp(distance * (-1.0 / kernel_reach)) * (scales[:, None] * scales[None, :])
    diagonal = jax.random.uniform(diagonal_key, (matrix_order,), jnp.float32, diagonal_low, diagonal_high)
    return kernel + jnp.diag(diagonal)


def draw_entries(key, part):
    key = jax.random.fold_in(key, 1)
    block_keys = jax.random.split(key, LEVELS * LEAVES)
    point_power, scale_low, scale_high = (1.0, 0.7, 1.3)

    def one_block(block_key):
        return kernel_matrix(block_key, F, point_power, scale_low, scale_high, 0.5, 1.0)
    return lax.map(one_block, block_keys).reshape(LEVELS, LEAVES, F, F)


def draw_child_update(key, part):
    key = jax.random.fold_in(key, 2)
    block_keys = jax.random.split(key, LEAVES)
    point_power, scale_low, scale_high = (1.0, 0.7, 1.3)

    def one_block(block_key):
        return kernel_matrix(block_key, U, point_power, scale_low, scale_high, 1.0, 2.0)
    return lax.map(one_block, block_keys)


def draw_slots(key, part):
    key = jax.random.fold_in(key, 3)
    block_keys = jax.random.split(key, LEVELS * LEAVES)
    shuffled = jax.vmap(lambda block_key: jax.random.permutation(block_key, F))(block_keys).astype(jnp.int32)
    placed = jnp.where(shuffled < U, shuffled, -1).astype(jnp.int32)
    return placed.reshape(LEVELS, LEAVES, F)


def setup_inputs(seed: int = 0) -> dict:
    keys = jax.random.split(jax.random.key(seed), 4)
    return {
        "child_update": draw_child_update(jax.random.fold_in(keys[3], 71), 0),
        "entries": draw_entries(jax.random.fold_in(keys[3], 71), 0),
        "slots": draw_slots(jax.random.fold_in(keys[3], 71), 0),
    }


def solve_block(pivot_block, coupling):
    factor = jnp.linalg.cholesky(pivot_block)
    partial_solve = lax.linalg.triangular_solve(factor, coupling, left_side=False, lower=True, transpose_a=True)
    return lax.linalg.triangular_solve(factor, partial_solve, left_side=False, lower=True, transpose_a=False)

def extend(update_block, slot_row):
    present = (slot_row >= 0).astype(update_block.dtype)
    source = jnp.maximum(slot_row, 0).astype(jnp.int32)
    widened = jnp.take(jnp.take(update_block, source, axis=0), source, axis=1)
    return widened * present[:, None] * present[None, :]

def eliminate(front_matrix):
    blocks = jnp.arange(N_FRONT, dtype=jnp.int32)[:, None] * ROWS
    pivot_index = (blocks + jnp.arange(PIVB, dtype=jnp.int32)[None, :]).reshape(-1)
    update_index = (blocks + jnp.arange(PIVB, ROWS, dtype=jnp.int32)[None, :]).reshape(-1)
    update_rows = jnp.take(front_matrix, update_index, axis=0)
    pivot_block = jnp.take(jnp.take(front_matrix, pivot_index, axis=0), pivot_index, axis=1)
    coupling = jnp.take(update_rows, pivot_index, axis=1)
    remainder = jnp.take(update_rows, update_index, axis=1)
    multiplier = solve_block(pivot_block, coupling)
    schur_part = remainder - jnp.dot(multiplier.astype(jnp.float32), coupling.T.astype(jnp.float32), precision=lax.Precision.HIGHEST, preferred_element_type=jnp.float32)
    return (multiplier, schur_part)

def reference(child_update, entries, slots):
    holdings = [child_update[member] for member in range(LEAVES)]
    multiplier_table = [[None] * LEVELS for member in range(LEAVES)]
    for level_index in range(LEVELS):
        group_size = 2 ** (level_index + 1)
        child_span = 2 ** level_index
        for first_leaf in range(0, LEAVES, group_size):
            assembled = entries[level_index, first_leaf]
            for member in range(first_leaf + 1, first_leaf + group_size):
                assembled = assembled + entries[level_index, member]
            for child_leaf in (first_leaf, first_leaf + child_span):
                assembled = assembled + extend(holdings[child_leaf], slots[level_index, child_leaf])
            multiplier, schur_part = eliminate(assembled)
            for member in range(first_leaf, first_leaf + group_size):
                multiplier_table[member][level_index] = multiplier
                holdings[member] = schur_part
    stacked = jnp.stack([jnp.stack(row_list) for row_list in multiplier_table])
    return (stacked, holdings[0])
```

```python
import functools

import jax
import jax.numpy as jnp
from jax import lax
from jax.experimental import pallas as pl
from jax.experimental.pallas import tpu as pltpu
from jax.sharding import Mesh, PartitionSpec as P

F32 = jnp.float32
HIGHEST = lax.Precision.HIGHEST
BLOCK = 128
PIV = 8
UPD = BLOCK - PIV
NF = 32
F = NF * BLOCK
NP = NF * PIV
VMEM_LIMIT = 48 << 20
LEAF = ("zl", "core")
FRONT = ("x", "y", "zh")


def vmem():
    return pl.BlockSpec(memory_space=pltpu.VMEM)


def smem():
    return pl.BlockSpec(memory_space=pltpu.SMEM)


def send_kernel(rows, cols, per, idx_ref, mask_ref, src_ref, out_ref, t_ref, g_ref):
    step = pl.program_id(0)

    @pl.when(step == 0)
    def _():
        for b in range(cols // BLOCK):
            blk = src_ref[:, b * BLOCK:(b + 1) * BLOCK]
            if rows < BLOCK:
                blk = jnp.concatenate([blk, jnp.zeros((BLOCK - rows, BLOCK), F32)], 0)
            t_ref[b * BLOCK:(b + 1) * BLOCK, :] = blk.T

    for j in range(per):
        base = (step * per + j) * BLOCK
        for k in range(BLOCK):
            g_ref[k:k + 1, :] = t_ref[pl.ds(idx_ref[base + k], 1), :]
        here = mask_ref[pl.ds(step * per + j, 1), :]
        out_ref[j] = jnp.where(here > 0, g_ref[...].T[:rows], 0.0)


def send(idx, mask, src):
    rows, cols = src.shape
    per = 4
    return pl.pallas_call(
        functools.partial(send_kernel, rows, cols, per),
        grid=(NF // per,),
        out_shape=jax.ShapeDtypeStruct((NF, rows, BLOCK), F32),
        in_specs=[smem(), vmem(), vmem()],
        out_specs=pl.BlockSpec((per, rows, BLOCK), lambda i: (i, 0, 0)),
        scratch_shapes=[pltpu.VMEM((cols, BLOCK), F32), pltpu.VMEM((BLOCK, BLOCK), F32)],
        compiler_params=pltpu.CompilerParams(vmem_limit_bytes=VMEM_LIMIT),
        name="send",
    )(idx, mask, src)


def recv_kernel(per, idx_ref, mask_ref, y_ref, e_ref, a_ref, p_ref, g_ref):
    step = pl.program_id(0)
    for j in range(per):
        base = (step * per + j) * BLOCK
        for k in range(BLOCK):
            g_ref[k:k + 1, :] = y_ref[pl.ds(idx_ref[base + k], 1), :]
        here = mask_ref[pl.ds(step * per + j, 1), :]
        c = slice(j * BLOCK, (j + 1) * BLOCK)
        blk = jnp.where(here > 0, g_ref[...].T, 0.0) + e_ref[0, 0, :, c]
        a_ref[:, c] = blk
        p_ref[j * PIV:(j + 1) * PIV, :] = blk.T[:PIV]


def recv(level, idx, mask, y, entries):
    per = 4
    return pl.pallas_call(
        functools.partial(recv_kernel, per),
        grid=(NF // per,),
        out_shape=[jax.ShapeDtypeStruct((BLOCK, F), F32), jax.ShapeDtypeStruct((NP, BLOCK), F32)],
        in_specs=[
            smem(),
            vmem(),
            vmem(),
            pl.BlockSpec((1, 1, BLOCK, per * BLOCK), lambda i: (level, 0, 0, i)),
        ],
        out_specs=[
            pl.BlockSpec((BLOCK, per * BLOCK), lambda i: (0, i)),
            pl.BlockSpec((per * PIV, BLOCK), lambda i: (i, 0)),
        ],
        scratch_shapes=[pltpu.VMEM((BLOCK, BLOCK), F32)],
        compiler_params=pltpu.CompilerParams(vmem_limit_bytes=VMEM_LIMIT),
        name="recv",
    )(idx, mask, y, entries)


def inv_small(D, n):
    rows = lax.broadcasted_iota(jnp.int32, (n, n), 0)
    cols = lax.broadcasted_iota(jnp.int32, (n, n), 1)
    lane = lax.broadcasted_iota(jnp.int32, (1, n), 1)
    for k in range(n):
        d = 1.0 / D[k:k + 1, k:k + 1]
        col = D[:, k:k + 1]
        row = jnp.where(lane == k, d, D[k:k + 1, :] * d)
        D = jnp.where(rows == k, row, jnp.where(cols == k, 0.0, D) - col * row)
    return D


def inv_kernel(nb, a_ref, o_ref):
    o_ref[...] = a_ref[...]
    for b in range(NP // nb):
        lo = b * nb
        Ab = o_ref[:, lo:lo + nb]
        Dinv = inv_small(Ab[lo:lo + nb, :], nb)
        lane = lax.broadcasted_iota(jnp.int32, (nb, NP), 1)
        eye = (lane - lo == lax.broadcasted_iota(jnp.int32, (nb, NP), 0)).astype(F32)
        Rb = jnp.where((lane >= lo) & (lane < lo + nb), eye, o_ref[lo:lo + nb, :])
        Rn = jnp.dot(Dinv, Rb, precision=HIGHEST, preferred_element_type=F32)
        lane2 = lax.broadcasted_iota(jnp.int32, (NP, NP), 1)
        rest = jnp.where((lane2 >= lo) & (lane2 < lo + nb), 0.0, o_ref[...])
        o_ref[...] = rest - jnp.dot(Ab, Rn, precision=HIGHEST, preferred_element_type=F32)
        o_ref[lo:lo + nb, :] = Rn


def inverse(a):
    return pl.pallas_call(
        functools.partial(inv_kernel, 64),
        out_shape=jax.ShapeDtypeStruct((NP, NP), F32),
        in_specs=[vmem()],
        out_specs=vmem(),
        compiler_params=pltpu.CompilerParams(vmem_limit_bytes=VMEM_LIMIT),
        name="inverse",
    )(a)


def swap(x, axis, d):
    n = lax.axis_size(axis)
    return lax.ppermute(x, axis, [(i, i ^ d) for i in range(n)])


def pick(x, i, dim):
    return lax.dynamic_index_in_dim(x, i, dim, keepdims=False)


def ordered(bit, mine, other, dim):
    first = jnp.where(bit == 0, mine, other)
    second = jnp.where(bit == 0, other, mine)
    return jnp.stack([first, second], dim)


def gather_front(x):
    zh = lax.axis_index("zh")
    both = ordered(zh, x, swap(x, "zh", 1), 0)
    out = jnp.broadcast_to(both[None], (NF // 2,) + both.shape)
    got = lax.all_to_all(out, ("x", "y"), split_axis=0, concat_axis=0, tiled=True)
    return got.reshape((NF * x.shape[0],) + x.shape[1:])


def shards(child_update, entries, slots):
    zl = lax.axis_index("zl")
    core = lax.axis_index("core")
    leaf = zl * 2 + core
    bits = [(core, "core", 1), (zl & 1, "zl", 1), (zl >> 1, "zl", 2)]
    src = child_update[0]
    mults = []
    S = None
    for t in range(3):
        slot = lax.dynamic_index_in_dim(slots[t], (leaf >> t) << t, 0, keepdims=False)
        present = slot >= 0
        at = jnp.maximum(slot, 0)
        if t == 0:
            col_idx = at
            row_idx = at
            mine = present
            src = child_update[0]
        else:
            blk, pos = at // UPD, at % UPD + PIV
            col_idx = blk * BLOCK + pos
            if t == 1:
                part = 64
                r = core
                s3 = S.reshape(2, 64, F // 2)
                got = swap(pick(s3, 1 - core, 0), "core", 1)
                src = ordered(core, pick(s3, core, 0), got, 1).reshape(64, F)
            else:
                part = 32
                z0 = zl & 1
                r = z0 * 2 + core
                s3 = S.reshape(2, 2, 32, F // 4)
                got = swap(pick(s3, 1 - z0, 0), "zl", 1)
                wide = ordered(z0, pick(s3, z0, 0), got, 2)
                got = swap(pick(wide, 1 - core, 0), "core", 1)
                src = ordered(core, pick(wide, core, 0), got, 2).reshape(32, F)
            mine = present & (pos // part == r)
            row_idx = jnp.where(mine, blk * part + pos - part * r, 0)
        as_mask = lambda m: m.astype(F32).reshape(NF, BLOCK)
        out = send(col_idx, as_mask(present), src)
        got = lax.all_to_all(out, FRONT, split_axis=0, concat_axis=0, tiled=True)
        A, pT = recv(t, row_idx, as_mask(mine), got.reshape(-1, BLOCK), entries)
        n = t + 1
        for k in range(n):
            bit, axis, d = bits[k]
            width = F >> (n - 0)
            a4 = A.reshape(BLOCK, 1 << (n - 1 - k), 2, width)
            away = swap(pick(a4, 1 - bit, 2), axis, d)
            A = (pick(a4, bit, 2) + away).reshape(BLOCK, -1)
            pT = pT + swap(pT, axis, d)
        panel = pT.T
        W = A.shape[1]
        got = gather_front(jnp.concatenate([panel[:PIV], A[:PIV]], 1))
        Ainv = inverse(got[:, :NP])
        M = jnp.dot(panel, Ainv, precision=HIGHEST, preferred_element_type=F32)
        S = A - jnp.dot(M, got[:, NP:], precision=HIGHEST, preferred_element_type=F32)
        mults.append(M[PIV:])
    top = S[PIV:].reshape(UPD, -1, BLOCK)[:, :, PIV:].reshape(UPD, -1)
    return jnp.stack(mults)[None], top


def solution(mesh):
    fine = Mesh(mesh.devices.reshape(4, 2, 4, 4, 2), LEAF + FRONT)
    in_specs = (P(LEAF, FRONT, None), P(None, LEAF, FRONT, None), P())
    out_specs = (P(LEAF, None, FRONT, None), P(FRONT, LEAF))
    return jax.shard_map(shards, mesh=fine, in_specs=in_specs, out_specs=out_specs, check_vma=False)
```

```python
import functools

import jax
import jax.numpy as jnp
from jax import lax
from jax.experimental import pallas as pl
from jax.experimental.pallas import tpu as pltpu
from jax.sharding import Mesh, PartitionSpec as P

F32 = jnp.float32
HIGHEST = lax.Precision.HIGHEST
BLOCK = 128
PIV = 8
UPD = BLOCK - PIV
NF = 32
F = NF * BLOCK
NP = NF * PIV
PER = 4
UNIT = PER * BLOCK
VMEM_LIMIT = 48 << 20
LEAF = ("zl", "core")
FRONT = ("x", "y", "zh")


def vmem():
    return pl.BlockSpec(memory_space=pltpu.VMEM)


def smem():
    return pl.BlockSpec(memory_space=pltpu.SMEM)


def params():
    return pltpu.CompilerParams(vmem_limit_bytes=VMEM_LIMIT)


def dot(a, b):
    return jnp.dot(a, b, precision=HIGHEST, preferred_element_type=F32)


def send_kernel(rows, cols, idx_ref, mask_ref, src_ref, out_ref, t_ref, g_ref):
    step = pl.program_id(0)

    @pl.when(step == 0)
    def _():
        for b in range(cols // BLOCK):
            blk = src_ref[:, b * BLOCK:(b + 1) * BLOCK]
            if rows < BLOCK:
                blk = jnp.concatenate([blk, jnp.zeros((BLOCK - rows, BLOCK), F32)], 0)
            t_ref[b * BLOCK:(b + 1) * BLOCK, :] = blk.T

    for j in range(PER):
        base = (step * PER + j) * BLOCK
        for k in range(BLOCK):
            g_ref[k:k + 1, :] = t_ref[pl.ds(idx_ref[base + k], 1), :]
        here = mask_ref[pl.ds(step * PER + j, 1), :]
        out_ref[j] = jnp.where(here > 0, g_ref[...].T[:rows], 0.0)


def send(idx, mask, src):
    rows, cols = src.shape
    return pl.pallas_call(
        functools.partial(send_kernel, rows, cols),
        grid=(NF // PER,),
        out_shape=jax.ShapeDtypeStruct((NF, rows, BLOCK), F32),
        in_specs=[smem(), vmem(), vmem()],
        out_specs=pl.BlockSpec((PER, rows, BLOCK), lambda i: (i, 0, 0)),
        scratch_shapes=[pltpu.VMEM((cols, BLOCK), F32), pltpu.VMEM((BLOCK, BLOCK), F32)],
        compiler_params=params(),
        name="send",
    )(idx, mask, src)


def place_pivots(idx_ref, mask_ref, y_ref, ep_ref, p_ref, g_ref):
    for j in range(NP // BLOCK):
        for k in range(BLOCK):
            g_ref[k:k + 1, :] = y_ref[pl.ds(idx_ref[j * BLOCK + k], 1), :]
        c = slice(j * BLOCK, (j + 1) * BLOCK)
        p_ref[:, c] = jnp.where(mask_ref[j:j + 1, :] > 0, g_ref[...].T, 0.0) + ep_ref[:, c]


def panel_kernel(idx_ref, mask_ref, y_ref, ep_ref, p_ref, g_ref):
    place_pivots(idx_ref, mask_ref, y_ref, ep_ref, p_ref, g_ref)


def panel(idx, mask, y, ep):
    return pl.pallas_call(
        panel_kernel,
        out_shape=jax.ShapeDtypeStruct((BLOCK, NP), F32),
        in_specs=[smem(), vmem(), vmem(), vmem()],
        out_specs=vmem(),
        scratch_shapes=[pltpu.VMEM((BLOCK, BLOCK), F32)],
        compiler_params=params(),
        name="panel",
    )(idx, mask, y, ep)


def correct_kernel(part, idx_ref, mask_ref, y_ref, ep_ref, got_ref, sel_ref, inv_ref, yc_ref, p_ref, g_ref, m_ref):
    m_ref[...] = dot(sel_ref[...], inv_ref[...]).T

    @pl.loop(0, NF // 2)
    def _(f):
        lhs = jnp.concatenate([got_ref[2 * f, :part, :], got_ref[2 * f + 1, :part, :]], 0)
        rows = pl.ds(pl.multiple_of(f * 2 * part, 2 * part), 2 * part)
        yc_ref[rows, :] = y_ref[rows, :] - dot(lhs, m_ref[...])

    place_pivots(idx_ref, mask_ref, yc_ref, ep_ref, p_ref, g_ref)


def correct(part, idx, mask, y, ep, got, sel, inv):
    return pl.pallas_call(
        functools.partial(correct_kernel, part),
        out_shape=[jax.ShapeDtypeStruct(y.shape, F32), jax.ShapeDtypeStruct((BLOCK, NP), F32)],
        in_specs=[smem()] + [vmem()] * 6,
        out_specs=[vmem(), vmem()],
        scratch_shapes=[pltpu.VMEM((BLOCK, BLOCK), F32), pltpu.VMEM((NP, BLOCK), F32)],
        compiler_params=params(),
        name="correct",
    )(idx, mask, y, ep, got, sel, inv)


def unit_of(level, i, core):
    if level == 0:
        return core * 4 + i
    if level == 1:
        return (i // 2) * 4 + core * 2 + i % 2
    return (i % 2) * 4 + (i // 2) * 2 + core


def recv_kernel(level, core_ref, idx_ref, mask_ref, y_ref, e_ref, a_ref, g_ref):
    unit = unit_of(level, pl.program_id(0), core_ref[0])
    for j in range(PER):
        base = (unit * PER + j) * BLOCK
        for k in range(BLOCK):
            g_ref[k:k + 1, :] = y_ref[pl.ds(idx_ref[base + k], 1), :]
        here = mask_ref[pl.ds(unit * PER + j, 1), :]
        c = slice(j * BLOCK, (j + 1) * BLOCK)
        a_ref[:, c] = jnp.where(here > 0, g_ref[...].T, 0.0) + e_ref[0, 0, :, c]


def recv(level, core, idx, mask, y, entries):
    return pl.pallas_call(
        functools.partial(recv_kernel, level),
        grid_spec=pltpu.PrefetchScalarGridSpec(
            num_scalar_prefetch=2,
            grid=(F // UNIT // 2,),
            in_specs=[
                vmem(),
                vmem(),
                pl.BlockSpec((1, 1, BLOCK, UNIT), lambda i, c, s: (level, 0, 0, unit_of(level, i, c[0]))),
            ],
            out_specs=pl.BlockSpec((BLOCK, UNIT), lambda i, c, s: (0, i)),
            scratch_shapes=[pltpu.VMEM((BLOCK, BLOCK), F32)],
        ),
        out_shape=jax.ShapeDtypeStruct((BLOCK, F // 2), F32),
        compiler_params=params(),
        name="recv",
    )(core, idx, mask, y, entries)


def inv_small(D, n):
    rows = lax.broadcasted_iota(jnp.int32, (n, n), 0)
    cols = lax.broadcasted_iota(jnp.int32, (n, n), 1)
    lane = lax.broadcasted_iota(jnp.int32, (1, n), 1)
    for k in range(n):
        d = 1.0 / D[k:k + 1, k:k + 1]
        col = D[:, k:k + 1]
        row = jnp.where(lane == k, d, D[k:k + 1, :] * d)
        D = jnp.where(rows == k, row, jnp.where(cols == k, 0.0, D) - col * row)
    return D


def inv_kernel(nb, a_ref, o_ref):
    o_ref[...] = a_ref[...].reshape(NP, NP)
    for b in range(NP // nb):
        lo = b * nb
        Ab = o_ref[:, lo:lo + nb]
        Dinv = inv_small(Ab[lo:lo + nb, :], nb)
        lane = lax.broadcasted_iota(jnp.int32, (nb, NP), 1)
        eye = (lane - lo == lax.broadcasted_iota(jnp.int32, (nb, NP), 0)).astype(F32)
        Rb = jnp.where((lane >= lo) & (lane < lo + nb), eye, o_ref[lo:lo + nb, :])
        Rn = dot(Dinv, Rb)
        lane2 = lax.broadcasted_iota(jnp.int32, (NP, NP), 1)
        rest = jnp.where((lane2 >= lo) & (lane2 < lo + nb), 0.0, o_ref[...])
        o_ref[...] = rest - dot(Ab, Rn)
        o_ref[lo:lo + nb, :] = Rn


def inverse(got):
    last = got.shape[1] // PIV - 1
    return pl.pallas_call(
        functools.partial(inv_kernel, 64),
        grid=(1,),
        out_shape=jax.ShapeDtypeStruct((NP, NP), F32),
        in_specs=[pl.BlockSpec((NF, PIV, NP), lambda i: (0, last, 0))],
        out_specs=pl.BlockSpec((NP, NP), lambda i: (0, 0)),
        compiler_params=params(),
        cost_estimate=pl.CostEstimate(flops=2 * 10**9, bytes_accessed=60 * 10**6, transcendentals=0),
        name="inverse",
    )(got)


def last_kernel(a_ref, a12_ref, p_ref, inv_ref, m0_ref, m1_ref, mult_ref, top_ref):
    m = dot(p_ref[...], inv_ref[...])
    mult_ref[0] = m0_ref[PIV:, :]
    mult_ref[1] = m1_ref[PIV:, :]
    mult_ref[2] = m[PIV:, :]
    a12 = a12_ref[...].reshape(NP, UNIT)
    s = a_ref[...] - dot(m, a12)
    for j in range(PER):
        top_ref[:, j * UPD:(j + 1) * UPD] = s[PIV:, j * BLOCK + PIV:(j + 1) * BLOCK]


def last(a, a12, p, inv, m0, m1):
    return pl.pallas_call(
        last_kernel,
        out_shape=[jax.ShapeDtypeStruct((3, UPD, NP), F32), jax.ShapeDtypeStruct((UPD, PER * UPD), F32)],
        in_specs=[vmem()] * 6,
        out_specs=[vmem(), vmem()],
        compiler_params=params(),
        name="last",
    )(a, a12, p, inv, m0, m1)


def swap(x, axis, d):
    n = lax.axis_size(axis)
    return lax.ppermute(x, axis, [(i, i ^ d) for i in range(n)])


def part_of(x, i, size, dim):
    return lax.dynamic_slice_in_dim(x, i * size, size, dim)


def ordered(bit, mine, other):
    return jnp.where(bit == 0, mine, other), jnp.where(bit == 0, other, mine)


def gather_front(x):
    both = jnp.stack(ordered(lax.axis_index("zh"), x, swap(x, "zh", 1)))
    out = jnp.broadcast_to(both[None], (NF // 2,) + both.shape)
    got = lax.all_to_all(out, ("x", "y"), split_axis=0, concat_axis=0, tiled=True)
    return got.reshape((NF,) + x.shape)


def shards(child_update, entries, slots):
    zl = lax.axis_index("zl")
    core = lax.axis_index("core")
    z0, z1 = zl & 1, zl >> 1
    front = lax.axis_index("x") * 8 + lax.axis_index("y") * 2 + lax.axis_index("zh")
    leaf = zl * 2 + core
    bits = [(core, "core", 1), (z0, "zl", 1), (z1, "zl", 2)]
    parts = [None, 64, 32]
    splits = [None, core, z0 * 2 + core]

    plans = []
    for t in range(3):
        slot = lax.dynamic_index_in_dim(slots[t], (leaf >> t) << t, 0, keepdims=False)
        present = slot >= 0
        at = jnp.maximum(slot, 0)
        plan = {}
        if t == 0:
            col, row, mine = at, at, present
        else:
            blk, pos = at // UPD, at % UPD + PIV
            part, r = parts[t], splits[t]
            col = blk * BLOCK + pos
            mine = present & (pos // part == r)
            row = jnp.where(mine, blk * part + pos - part * r, 0)
            sel_row = jnp.where(mine, blk * (part + PIV) + pos - part * r, 0)
            plan["sel"] = part_of(sel_row, front, BLOCK, 0)
            plan["sel_mask"] = part_of(mine, front, BLOCK, 0).astype(F32)[:, None]
        plan["col"] = col
        plan["col_mask"] = present.astype(F32).reshape(NF, BLOCK)
        plan["row"] = row
        plan["row_mask"] = mine.astype(F32).reshape(NF, BLOCK)
        plan["piv"] = row.reshape(NF, BLOCK)[:, :PIV].reshape(NP)
        plan["piv_mask"] = plan["row_mask"][:, :PIV].reshape(NP // BLOCK, BLOCK)
        plan["ep"] = entries[t, 0].reshape(BLOCK, NF, BLOCK)[:, :, :PIV].reshape(BLOCK, NP)
        plans.append(plan)
    here, there = core.reshape(1), (1 - core).reshape(1)

    mults = []
    src = child_update[0]
    got = inv = sel = None
    for t in range(3):
        plan = plans[t]
        out = send(plan["col"], plan["col_mask"], src)
        y = lax.all_to_all(out, FRONT, split_axis=0, concat_axis=0, tiled=True).reshape(-1, BLOCK)
        if t == 0:
            y, plans = lax.optimization_barrier((y, plans))
            plan = plans[0]
            p = panel(plan["piv"], plan["piv_mask"], y, plan["ep"])
        else:
            y, p = correct(parts[t], plan["piv"], plan["piv_mask"], y, plan["ep"], got, sel, inv)
        for bit, axis, d in bits[:t + 1]:
            p = p + swap(p, axis, d)
        away = recv(t, there, plan["row"], plan["row_mask"], y, entries)
        moved = swap(away, "core", 1)
        A = recv(t, here, plan["row"], plan["row_mask"], y, entries) + moved
        for bit, axis, d in bits[1:t + 1]:
            half = A.shape[1] // 2
            A = part_of(A, bit, half, 1) + swap(part_of(A, 1 - bit, half, 1), axis, d)
        if t == 2:
            break
        part, r = parts[t + 1], splits[t + 1]
        nxt = plans[t + 1]
        got = gather_front(jnp.concatenate([part_of(p, r, part, 0), p[:PIV]], 0))
        flat = got.reshape(-1, NP)
        sel = jnp.take(flat, nxt["sel"], axis=0) * nxt["sel_mask"]
        for bit, axis, d in bits[:t + 1]:
            sel = sel + swap(sel, axis, d)
        inv = inverse(got)
        mults.append(dot(p, inv))
        if t == 0:
            mine = part_of(A, core, 64, 0)
            src = jnp.concatenate(ordered(core, mine, swap(part_of(A, 1 - core, 64, 0), "core", 1)), 1)
        else:
            mine = part_of(A, z0, 64, 0)
            wide = ordered(z0, mine, swap(part_of(A, 1 - z0, 64, 0), "zl", 1))
            wide = jnp.concatenate(wide, 1)
            mine = part_of(wide, core, 32, 0)
            lo, hi = ordered(core, mine, swap(part_of(wide, 1 - core, 32, 0), "core", 1))
            w = F // 4
            src = jnp.concatenate([lo[:, :w], hi[:, :w], lo[:, w:], hi[:, w:]], 1)
    inv = inverse(gather_front(p[:PIV]))
    a12 = gather_front(A[:PIV])
    mult, top = last(A, a12, p, inv, *mults)
    return mult[None], top


def solution(mesh):
    fine = Mesh(mesh.devices.reshape(4, 2, 4, 4, 2), LEAF + FRONT)
    in_specs = (P(LEAF, FRONT, None), P(None, LEAF, FRONT, None), P())
    out_specs = (P(LEAF, None, FRONT, None), P(FRONT, LEAF))
    return jax.shard_map(shards, mesh=fine, in_specs=in_specs, out_specs=out_specs, check_vma=False)
```

```python
import functools

import jax
import jax.numpy as jnp
from jax import lax
from jax.experimental import pallas as pl
from jax.experimental.pallas import tpu as pltpu
from jax.sharding import Mesh, PartitionSpec as P

F32 = jnp.float32
HIGHEST = lax.Precision.HIGHEST
BLOCK = 128
PIV = 8
UPD = BLOCK - PIV
NF = 32
F = NF * BLOCK
NP = NF * PIV
PER = 4
UNIT = PER * BLOCK
VMEM_LIMIT = 48 << 20
LEAF = ("zl", "core")
FRONT = ("x", "y", "zh")


def vmem():
    return pl.BlockSpec(memory_space=pltpu.VMEM)


def smem():
    return pl.BlockSpec(memory_space=pltpu.SMEM)


def params():
    return pltpu.CompilerParams(vmem_limit_bytes=VMEM_LIMIT)


def dot(a, b):
    return jnp.dot(a, b, precision=HIGHEST, preferred_element_type=F32)


def send_kernel(rows, cols, idx_ref, mask_ref, src_ref, out_ref, t_ref, g_ref):
    step = pl.program_id(0)

    @pl.when(step == 0)
    def _():
        for b in range(cols // BLOCK):
            blk = src_ref[:, b * BLOCK:(b + 1) * BLOCK]
            if rows < BLOCK:
                blk = jnp.concatenate([blk, jnp.zeros((BLOCK - rows, BLOCK), F32)], 0)
            t_ref[b * BLOCK:(b + 1) * BLOCK, :] = blk.T

    for j in range(PER):
        base = (step * PER + j) * BLOCK
        for k in range(BLOCK):
            g_ref[k:k + 1, :] = t_ref[pl.ds(idx_ref[base + k], 1), :]
        here = mask_ref[pl.ds(step * PER + j, 1), :]
        out_ref[j] = jnp.where(here > 0, g_ref[...].T[:rows], 0.0)


def send(idx, mask, src):
    rows, cols = src.shape
    return pl.pallas_call(
        functools.partial(send_kernel, rows, cols),
        grid=(NF // PER,),
        out_shape=jax.ShapeDtypeStruct((NF, rows, BLOCK), F32),
        in_specs=[smem(), vmem(), vmem()],
        out_specs=pl.BlockSpec((PER, rows, BLOCK), lambda i: (i, 0, 0)),
        scratch_shapes=[pltpu.VMEM((cols, BLOCK), F32), pltpu.VMEM((BLOCK, BLOCK), F32)],
        compiler_params=params(),
        name="send",
    )(idx, mask, src)


def place_pivots(idx_ref, y_ref, g_ref):
    for k in range(NP):
        g_ref[k:k + 1, :] = y_ref[pl.ds(idx_ref[k], 1), :]


def store_pivots(rows, mask_ref, ep_ref, p_ref, q_ref):
    for j in range(NP // BLOCK):
        c = slice(j * BLOCK, (j + 1) * BLOCK)
        blk = jnp.where(mask_ref[j:j + 1, :] > 0, rows[c].T, 0.0) + ep_ref[:, c]
        p_ref[:, c] = blk
        q_ref[:, c] = blk[:PIV]


def panel_kernel(idx_ref, mask_ref, y_ref, ep_ref, p_ref, q_ref, g_ref):
    place_pivots(idx_ref, y_ref, g_ref)
    store_pivots(g_ref[...], mask_ref, ep_ref, p_ref, q_ref)


def panel_less_kernel(idx_ref, mask_ref, y_ref, ep_ref, got_ref, sel_ref, inv_ref, p_ref, q_ref, g_ref, h_ref):
    place_pivots(idx_ref, y_ref, g_ref)
    place_pivots(idx_ref, got_ref, h_ref)
    rows = g_ref[...] - dot(h_ref[...], dot(sel_ref[...], inv_ref[...]).T)
    store_pivots(rows, mask_ref, ep_ref, p_ref, q_ref)


def panel(idx, mask, y, ep, child=()):
    return pl.pallas_call(
        panel_less_kernel if child else panel_kernel,
        out_shape=[jax.ShapeDtypeStruct((BLOCK, NP), F32), jax.ShapeDtypeStruct((PIV, NP), F32)],
        in_specs=[smem()] + [vmem()] * (3 + len(child)),
        out_specs=[vmem(), vmem()],
        scratch_shapes=[pltpu.VMEM((NP, BLOCK), F32)] + [pltpu.VMEM((NP, NP), F32)] * (1 if child else 0),
        compiler_params=params(),
        name="panel",
    )(idx, mask, y, ep, *child)


def correct_kernel(y_ref, got_ref, sel_ref, inv_ref, yc_ref, m_ref):
    @pl.when(pl.program_id(0) == 0)
    def _():
        m_ref[...] = dot(sel_ref[...], inv_ref[...]).T

    yc_ref[...] = y_ref[...] - dot(got_ref[...], m_ref[...])


def correct(y, got, sel, inv):
    rows = y.shape[0] // 4
    return pl.pallas_call(
        correct_kernel,
        grid=(4,),
        out_shape=jax.ShapeDtypeStruct(y.shape, F32),
        in_specs=[
            pl.BlockSpec((rows, BLOCK), lambda i: (i, 0)),
            pl.BlockSpec((rows, NP), lambda i: (i, 0)),
            vmem(),
            vmem(),
        ],
        out_specs=pl.BlockSpec((rows, BLOCK), lambda i: (i, 0)),
        scratch_shapes=[pltpu.VMEM((NP, BLOCK), F32)],
        compiler_params=params(),
        name="correct",
    )(y, got, sel, inv)


def unit_of(level, i, core):
    if level == 0:
        return core * 4 + i
    if level == 1:
        return (i // 2) * 4 + core * 2 + i % 2
    return (i % 2) * 4 + (i // 2) * 2 + core


def recv_kernel(level, core_ref, idx_ref, mask_ref, y_ref, e_ref, a_ref, g_ref):
    unit = unit_of(level, pl.program_id(0), core_ref[0])
    for j in range(PER):
        base = (unit * PER + j) * BLOCK
        for k in range(BLOCK):
            g_ref[k:k + 1, :] = y_ref[pl.ds(idx_ref[base + k], 1), :]
        here = mask_ref[pl.ds(unit * PER + j, 1), :]
        c = slice(j * BLOCK, (j + 1) * BLOCK)
        a_ref[:, c] = jnp.where(here > 0, g_ref[...].T, 0.0) + e_ref[0, 0, :, c]


def recv(level, core, idx, mask, y, entries):
    return pl.pallas_call(
        functools.partial(recv_kernel, level),
        grid_spec=pltpu.PrefetchScalarGridSpec(
            num_scalar_prefetch=2,
            grid=(F // UNIT // 2,),
            in_specs=[
                vmem(),
                vmem(),
                pl.BlockSpec((1, 1, BLOCK, UNIT), lambda i, c, s: (level, 0, 0, unit_of(level, i, c[0]))),
            ],
            out_specs=pl.BlockSpec((BLOCK, UNIT), lambda i, c, s: (0, i)),
            scratch_shapes=[pltpu.VMEM((BLOCK, BLOCK), F32)],
        ),
        out_shape=jax.ShapeDtypeStruct((BLOCK, F // 2), F32),
        compiler_params=params(),
        name="recv",
    )(core, idx, mask, y, entries)


def inv_small(D, n, step):
    rows = lax.broadcasted_iota(jnp.int32, (n, n), 0)
    cols = lax.broadcasted_iota(jnp.int32, (n, n), 1)
    lane = lax.broadcasted_iota(jnp.int32, (1, n), 1)
    for k in range(0, n, step):
        C = [jnp.broadcast_to(D[:, k + j:k + j + 1], (n, n)) for j in range(step)]
        B = [[C[j][k + i:k + i + 1, :] for j in range(step)] for i in range(step)]
        R = []
        for i in range(step):
            unit = jnp.where(lane == k + i, 1.0, 0.0)
            R.append(jnp.where((lane >= k) & (lane < k + step), unit, D[k + i:k + i + 1, :]))
        for p in range(step):
            d = 1.0 / B[p][p]
            for j in range(p + 1, step):
                B[p][j] = B[p][j] * d
            R[p] = R[p] * d
            for i in range(step):
                if i != p:
                    f = B[i][p]
                    for j in range(p + 1, step):
                        B[i][j] = B[i][j] - f * B[p][j]
                    R[i] = R[i] - f * R[p]
        D = jnp.where((cols >= k) & (cols < k + step), 0.0, D)
        for j in range(step):
            D = D - C[j] * R[j]
        for i in range(step):
            D = jnp.where(rows == k + i, R[i], D)
    return D


def inv_kernel(nb, a_ref, o_ref):
    o_ref[...] = a_ref[...].reshape(NP, NP)
    for b in range(NP // nb):
        lo = b * nb
        Ab = o_ref[:, lo:lo + nb]
        Dinv = inv_small(Ab[lo:lo + nb, :], nb, 8)
        lane = lax.broadcasted_iota(jnp.int32, (nb, NP), 1)
        eye = (lane - lo == lax.broadcasted_iota(jnp.int32, (nb, NP), 0)).astype(F32)
        Rb = jnp.where((lane >= lo) & (lane < lo + nb), eye, o_ref[lo:lo + nb, :])
        Rn = dot(Dinv, Rb)
        lane2 = lax.broadcasted_iota(jnp.int32, (NP, NP), 1)
        rest = jnp.where((lane2 >= lo) & (lane2 < lo + nb), 0.0, o_ref[...])
        o_ref[...] = rest - dot(Ab, Rn)
        o_ref[lo:lo + nb, :] = Rn


def inverse(got):
    return pl.pallas_call(
        functools.partial(inv_kernel, 64),
        out_shape=jax.ShapeDtypeStruct((NP, NP), F32),
        in_specs=[vmem()],
        out_specs=vmem(),
        compiler_params=params(),
        cost_estimate=pl.CostEstimate(flops=2 * 10**9, bytes_accessed=40 * 10**6, transcendentals=0),
        name="inverse",
    )(got)


def last_kernel(a_ref, a12_ref, p_ref, inv_ref, m0_ref, m1_ref, mult_ref, top_ref):
    m = dot(p_ref[...], inv_ref[...])
    mult_ref[0] = m0_ref[PIV:, :]
    mult_ref[1] = m1_ref[PIV:, :]
    mult_ref[2] = m[PIV:, :]
    a12 = a12_ref[...].reshape(NP, UNIT)
    s = a_ref[...] - dot(m, a12)
    for j in range(PER):
        top_ref[:, j * UPD:(j + 1) * UPD] = s[PIV:, j * BLOCK + PIV:(j + 1) * BLOCK]


def last(a, a12, p, inv, m0, m1):
    return pl.pallas_call(
        last_kernel,
        out_shape=[jax.ShapeDtypeStruct((3, UPD, NP), F32), jax.ShapeDtypeStruct((UPD, PER * UPD), F32)],
        in_specs=[vmem()] * 6,
        out_specs=[vmem(), vmem()],
        compiler_params=params(),
        name="last",
    )(a, a12, p, inv, m0, m1)


def swap(x, axis, d):
    n = lax.axis_size(axis)
    return lax.ppermute(x, axis, [(i, i ^ d) for i in range(n)])


def part_of(x, i, size, dim):
    return lax.dynamic_slice_in_dim(x, i * size, size, dim)


def ordered(bit, mine, other):
    return jnp.where(bit == 0, mine, other), jnp.where(bit == 0, other, mine)


def tie(x, y):
    return lax.optimization_barrier((x, y))


def both_halves(x):
    both = jnp.stack(ordered(lax.axis_index("zh"), x, swap(x, "zh", 1)))
    return jnp.broadcast_to(both[None], (NF // 2,) + both.shape)


def gather_xy(out):
    got = lax.all_to_all(out, ("x", "y"), split_axis=0, concat_axis=0, tiled=True)
    return got.reshape((NF,) + out.shape[2:])


def gather_all(x):
    out = jnp.broadcast_to(x[None], (NF,) + x.shape)
    return lax.all_to_all(out, FRONT, split_axis=0, concat_axis=0, tiled=True)


def shards(child_update, entries, slots):
    zl = lax.axis_index("zl")
    core = lax.axis_index("core")
    z0, z1 = zl & 1, zl >> 1
    front = lax.axis_index("x") * 8 + lax.axis_index("y") * 2 + lax.axis_index("zh")
    leaf = zl * 2 + core
    bits = [(core, "core", 1), (z0, "zl", 1), (z1, "zl", 2)]
    parts = [None, 64, 32]
    splits = [None, core, z0 * 2 + core]

    plans = []
    for t in range(3):
        slot = lax.dynamic_index_in_dim(slots[t], (leaf >> t) << t, 0, keepdims=False)
        present = slot >= 0
        at = jnp.maximum(slot, 0)
        plan = {}
        if t == 0:
            col, row, mine = at, at, present
        else:
            blk, pos = at // UPD, at % UPD + PIV
            part, r = parts[t], splits[t]
            col = blk * BLOCK + pos
            mine = present & (pos // part == r)
            row = jnp.where(mine, blk * part + pos - part * r, 0)
            plan["sel"] = part_of(row, front, BLOCK, 0)
            plan["sel_mask"] = part_of(mine, front, BLOCK, 0).astype(F32)[:, None]
        plan["col"] = col
        plan["col_mask"] = present.astype(F32).reshape(NF, BLOCK)
        plan["row"] = row
        plan["row_mask"] = mine.astype(F32).reshape(NF, BLOCK)
        plan["piv"] = row.reshape(NF, BLOCK)[:, :PIV].reshape(NP)
        plan["piv_mask"] = plan["row_mask"][:, :PIV].reshape(NP // BLOCK, BLOCK)
        plan["ep"] = entries[t, 0].reshape(BLOCK, NF, BLOCK)[:, :, :PIV].reshape(BLOCK, NP)
        plans.append(plan)
    here, there = core.reshape(1), (1 - core).reshape(1)

    mults = []
    src = child_update[0]
    child = ()
    prev = None
    for t in range(3):
        plan = plans[t]
        out = send(plan["col"], plan["col_mask"], src)
        if t:
            out, prev = tie(out, prev)
            child = (prev, sel, inv)
        y = lax.all_to_all(out, FRONT, split_axis=0, concat_axis=0, tiled=True).reshape(-1, BLOCK)
        if t == 0:
            y, plans = tie(y, plans)
            plan = plans[0]
        p, q = panel(plan["piv"], plan["piv_mask"], y, plan["ep"], child)
        for bit, axis, d in bits[:t + 1]:
            q = q + swap(q, axis, d)
        if t:
            y = correct(y, *child)
        away = recv(t, there, plan["row"], plan["row_mask"], y, entries)
        away, q = tie(away, q)
        gq = gather_all(q)
        for bit, axis, d in bits[:t + 1]:
            p = p + swap(p, axis, d)
        A = recv(t, here, plan["row"], plan["row_mask"], y, entries) + swap(away, "core", 1)
        for bit, axis, d in bits[1:t + 1]:
            half = A.shape[1] // 2
            A = part_of(A, bit, half, 1) + swap(part_of(A, 1 - bit, half, 1), axis, d)
        if t == 2:
            break
        part, r = parts[t + 1], splits[t + 1]
        nxt = plans[t + 1]
        out, gq = tie(both_halves(part_of(p, r, part, 0)), gq)
        prev = gather_xy(out).reshape(-1, NP)
        sel = jnp.take(prev, nxt["sel"], axis=0) * nxt["sel_mask"]
        for bit, axis, d in bits[:t + 1]:
            sel = sel + swap(sel, axis, d)
        inv = inverse(gq)
        mults.append(dot(p, inv))
        if t == 0:
            mine = part_of(A, core, 64, 0)
            src = jnp.concatenate(ordered(core, mine, swap(part_of(A, 1 - core, 64, 0), "core", 1)), 1)
        else:
            mine = part_of(A, z0, 64, 0)
            wide = ordered(z0, mine, swap(part_of(A, 1 - z0, 64, 0), "zl", 1))
            wide = jnp.concatenate(wide, 1)
            mine = part_of(wide, core, 32, 0)
            lo, hi = ordered(core, mine, swap(part_of(wide, 1 - core, 32, 0), "core", 1))
            w = F // 4
            src = jnp.concatenate([lo[:, :w], hi[:, :w], lo[:, w:], hi[:, w:]], 1)
    out, gq = tie(both_halves(A[:PIV]), gq)
    a12 = gather_xy(out)
    mult, top = last(A, a12, p, inverse(gq), *mults)
    return mult[None], top


def solution(mesh):
    fine = Mesh(mesh.devices.reshape(4, 2, 4, 4, 2), LEAF + FRONT)
    in_specs = (P(LEAF, FRONT, None), P(None, LEAF, FRONT, None), P())
    out_specs = (P(LEAF, None, FRONT, None), P(FRONT, LEAF))
    return jax.shard_map(shards, mesh=fine, in_specs=in_specs, out_specs=out_specs, check_vma=False)
```

```python
import functools

import jax
import jax.numpy as jnp
from jax import lax
from jax.experimental import pallas as pl
from jax.experimental.pallas import tpu as pltpu
from jax.sharding import Mesh, PartitionSpec as P

F32 = jnp.float32
HIGHEST = lax.Precision.HIGHEST
BLOCK = 128
PIV = 8
UPD = BLOCK - PIV
NF = 32
F = NF * BLOCK
NP = NF * PIV
PER = 4
UNIT = PER * BLOCK
VMEM_LIMIT = 48 << 20
LEAF = ("zl", "core")
FRONT = ("x", "y", "zh")


def vmem():
    return pl.BlockSpec(memory_space=pltpu.VMEM)


def smem():
    return pl.BlockSpec(memory_space=pltpu.SMEM)


def params():
    return pltpu.CompilerParams(vmem_limit_bytes=VMEM_LIMIT)


def dot(a, b):
    return jnp.dot(a, b, precision=HIGHEST, preferred_element_type=F32)


def send_kernel(rows, cols, idx_ref, mask_ref, src_ref, out_ref, t_ref, g_ref):
    step = pl.program_id(0)

    @pl.when(step == 0)
    def _():
        for b in range(cols // BLOCK):
            blk = src_ref[:, b * BLOCK:(b + 1) * BLOCK]
            if rows < BLOCK:
                blk = jnp.concatenate([blk, jnp.zeros((BLOCK - rows, BLOCK), F32)], 0)
            t_ref[b * BLOCK:(b + 1) * BLOCK, :] = blk.T

    for j in range(PER):
        base = (step * PER + j) * BLOCK
        for k in range(BLOCK):
            g_ref[k:k + 1, :] = t_ref[pl.ds(idx_ref[base + k], 1), :]
        here = mask_ref[pl.ds(step * PER + j, 1), :]
        out_ref[j] = jnp.where(here > 0, g_ref[...].T[:rows], 0.0)


def send(idx, mask, src):
    rows, cols = src.shape
    return pl.pallas_call(
        functools.partial(send_kernel, rows, cols),
        grid=(NF // PER,),
        out_shape=jax.ShapeDtypeStruct((NF, rows, BLOCK), F32),
        in_specs=[smem(), vmem(), vmem()],
        out_specs=pl.BlockSpec((PER, rows, BLOCK), lambda i: (i, 0, 0)),
        scratch_shapes=[pltpu.VMEM((cols, BLOCK), F32), pltpu.VMEM((BLOCK, BLOCK), F32)],
        compiler_params=params(),
        name="send",
    )(idx, mask, src)


def place_pivots(idx_ref, y_ref, g_ref):
    for k in range(NP):
        g_ref[k:k + 1, :] = y_ref[pl.ds(idx_ref[k], 1), :]


def store_pivots(rows, mask_ref, ep_ref, p_ref, q_ref):
    for j in range(NP // BLOCK):
        c = slice(j * BLOCK, (j + 1) * BLOCK)
        blk = jnp.where(mask_ref[j:j + 1, :] > 0, rows[c].T, 0.0) + ep_ref[:, c]
        p_ref[:, c] = blk
        q_ref[:, c] = blk[:PIV]


def panel_kernel(idx_ref, mask_ref, y_ref, ep_ref, p_ref, q_ref, g_ref):
    place_pivots(idx_ref, y_ref, g_ref)
    store_pivots(g_ref[...], mask_ref, ep_ref, p_ref, q_ref)


def panel_less_kernel(idx_ref, mask_ref, y_ref, ep_ref, jdx_ref, got_ref, sel_ref, inv_ref, p_ref, q_ref, g_ref, h_ref):
    place_pivots(idx_ref, y_ref, g_ref)
    place_pivots(jdx_ref, got_ref, h_ref)
    rows = g_ref[...] - dot(h_ref[...], dot(sel_ref[...], inv_ref[...]).T)
    store_pivots(rows, mask_ref, ep_ref, p_ref, q_ref)


def panel(idx, mask, y, ep, child=()):
    return pl.pallas_call(
        panel_less_kernel if child else panel_kernel,
        out_shape=[jax.ShapeDtypeStruct((BLOCK, NP), F32), jax.ShapeDtypeStruct((PIV, NP), F32)],
        in_specs=[smem()] + [vmem()] * 3 + ([smem()] + [vmem()] * 3 if child else []),
        out_specs=[vmem(), vmem()],
        scratch_shapes=[pltpu.VMEM((NP, BLOCK), F32)] + [pltpu.VMEM((NP, NP), F32)] * (1 if child else 0),
        compiler_params=params(),
        name="panel",
    )(idx, mask, y, ep, *child)


def correct_kernel(part, y_ref, got_ref, sel_ref, inv_ref, yc_ref, m_ref):
    @pl.when(pl.program_id(0) == 0)
    def _():
        m_ref[...] = dot(sel_ref[...], inv_ref[...]).T

    got = got_ref[:, :part, :].reshape(-1, NP)
    yc_ref[...] = y_ref[...] - dot(got, m_ref[...])


def correct(part, y, got, sel, inv):
    rows = y.shape[0] // 4
    return pl.pallas_call(
        functools.partial(correct_kernel, part),
        grid=(4,),
        out_shape=jax.ShapeDtypeStruct(y.shape, F32),
        in_specs=[
            pl.BlockSpec((rows, BLOCK), lambda i: (i, 0)),
            pl.BlockSpec((NF // 4, part + PIV, NP), lambda i: (i, 0, 0)),
            vmem(),
            vmem(),
        ],
        out_specs=pl.BlockSpec((rows, BLOCK), lambda i: (i, 0)),
        scratch_shapes=[pltpu.VMEM((NP, BLOCK), F32)],
        compiler_params=params(),
        name="correct",
    )(y, got, sel, inv)


def unit_of(level, i, core):
    if level == 0:
        return core * 4 + i
    if level == 1:
        return (i // 2) * 4 + core * 2 + i % 2
    return (i % 2) * 4 + (i // 2) * 2 + core


def recv_kernel(level, core_ref, idx_ref, mask_ref, y_ref, e_ref, a_ref, g_ref):
    unit = unit_of(level, pl.program_id(0), core_ref[0])
    for j in range(PER):
        base = (unit * PER + j) * BLOCK
        for k in range(BLOCK):
            g_ref[k:k + 1, :] = y_ref[pl.ds(idx_ref[base + k], 1), :]
        here = mask_ref[pl.ds(unit * PER + j, 1), :]
        c = slice(j * BLOCK, (j + 1) * BLOCK)
        a_ref[:, c] = jnp.where(here > 0, g_ref[...].T, 0.0) + e_ref[0, 0, :, c]


def recv(level, core, idx, mask, y, entries):
    return pl.pallas_call(
        functools.partial(recv_kernel, level),
        grid_spec=pltpu.PrefetchScalarGridSpec(
            num_scalar_prefetch=2,
            grid=(F // UNIT // 2,),
            in_specs=[
                vmem(),
                vmem(),
                pl.BlockSpec((1, 1, BLOCK, UNIT), lambda i, c, s: (level, 0, 0, unit_of(level, i, c[0]))),
            ],
            out_specs=pl.BlockSpec((BLOCK, UNIT), lambda i, c, s: (0, i)),
            scratch_shapes=[pltpu.VMEM((BLOCK, BLOCK), F32)],
        ),
        out_shape=jax.ShapeDtypeStruct((BLOCK, F // 2), F32),
        compiler_params=params(),
        name="recv",
    )(core, idx, mask, y, entries)


def inv_small(D, n, step):
    rows = lax.broadcasted_iota(jnp.int32, (n, n), 0)
    cols = lax.broadcasted_iota(jnp.int32, (n, n), 1)
    lane = lax.broadcasted_iota(jnp.int32, (1, n), 1)
    for k in range(0, n, step):
        C = [jnp.broadcast_to(D[:, k + j:k + j + 1], (n, n)) for j in range(step)]
        B = [[C[j][k + i:k + i + 1, :] for j in range(step)] for i in range(step)]
        R = []
        for i in range(step):
            unit = jnp.where(lane == k + i, 1.0, 0.0)
            R.append(jnp.where((lane >= k) & (lane < k + step), unit, D[k + i:k + i + 1, :]))
        for p in range(step):
            d = 1.0 / B[p][p]
            for j in range(p + 1, step):
                B[p][j] = B[p][j] * d
            R[p] = R[p] * d
            for i in range(step):
                if i != p:
                    f = B[i][p]
                    for j in range(p + 1, step):
                        B[i][j] = B[i][j] - f * B[p][j]
                    R[i] = R[i] - f * R[p]
        D = jnp.where((cols >= k) & (cols < k + step), 0.0, D)
        for j in range(step):
            D = D - C[j] * R[j]
        for i in range(step):
            D = jnp.where(rows == k + i, R[i], D)
    return D


def inv_kernel(nb, a_ref, o_ref):
    o_ref[...] = a_ref[...].reshape(NP, NP)
    for b in range(NP // nb):
        lo = b * nb
        Ab = o_ref[:, lo:lo + nb]
        Dinv = inv_small(Ab[lo:lo + nb, :], nb, 8)
        lane = lax.broadcasted_iota(jnp.int32, (nb, NP), 1)
        eye = (lane - lo == lax.broadcasted_iota(jnp.int32, (nb, NP), 0)).astype(F32)
        Rb = jnp.where((lane >= lo) & (lane < lo + nb), eye, o_ref[lo:lo + nb, :])
        Rn = dot(Dinv, Rb)
        lane2 = lax.broadcasted_iota(jnp.int32, (NP, NP), 1)
        rest = jnp.where((lane2 >= lo) & (lane2 < lo + nb), 0.0, o_ref[...])
        o_ref[...] = rest - dot(Ab, Rn)
        o_ref[lo:lo + nb, :] = Rn


def inverse(got):
    last = got.shape[1] // PIV - 1
    return pl.pallas_call(
        functools.partial(inv_kernel, 64),
        grid=(1,),
        out_shape=jax.ShapeDtypeStruct((NP, NP), F32),
        in_specs=[pl.BlockSpec((NF, PIV, NP), lambda i: (0, last, 0))],
        out_specs=pl.BlockSpec((NP, NP), lambda i: (0, 0)),
        compiler_params=params(),
        cost_estimate=pl.CostEstimate(flops=2 * 10**9, bytes_accessed=40 * 10**6, transcendentals=0),
        name="inverse",
    )(got)


def last_kernel(a_ref, a12_ref, p_ref, inv_ref, m0_ref, m1_ref, mult_ref, top_ref):
    m = dot(p_ref[...], inv_ref[...])
    mult_ref[0] = m0_ref[PIV:, :]
    mult_ref[1] = m1_ref[PIV:, :]
    mult_ref[2] = m[PIV:, :]
    a12 = a12_ref[...].reshape(NP, UNIT)
    s = a_ref[...] - dot(m, a12)
    for j in range(PER):
        top_ref[:, j * UPD:(j + 1) * UPD] = s[PIV:, j * BLOCK + PIV:(j + 1) * BLOCK]


def last(a, a12, p, inv, m0, m1):
    return pl.pallas_call(
        last_kernel,
        out_shape=[jax.ShapeDtypeStruct((3, UPD, NP), F32), jax.ShapeDtypeStruct((UPD, PER * UPD), F32)],
        in_specs=[vmem()] * 6,
        out_specs=[vmem(), vmem()],
        compiler_params=params(),
        name="last",
    )(a, a12, p, inv, m0, m1)


def swap(x, axis, d):
    n = lax.axis_size(axis)
    return lax.ppermute(x, axis, [(i, i ^ d) for i in range(n)])


def part_of(x, i, size, dim):
    return lax.dynamic_slice_in_dim(x, i * size, size, dim)


def ordered(bit, mine, other):
    return jnp.where(bit == 0, mine, other), jnp.where(bit == 0, other, mine)


def tie(x, y):
    return lax.optimization_barrier((x, y))


def both_halves(x):
    both = jnp.stack(ordered(lax.axis_index("zh"), x, swap(x, "zh", 1)))
    return jnp.broadcast_to(both[None], (NF // 2,) + both.shape)


def gather_xy(out):
    got = lax.all_to_all(out, ("x", "y"), split_axis=0, concat_axis=0, tiled=True)
    return got.reshape((NF,) + out.shape[2:])


def gather_all(x):
    out = jnp.broadcast_to(x[None], (NF,) + x.shape)
    return lax.all_to_all(out, FRONT, split_axis=0, concat_axis=0, tiled=True)


def shards(child_update, entries, slots):
    zl = lax.axis_index("zl")
    core = lax.axis_index("core")
    z0, z1 = zl & 1, zl >> 1
    front = lax.axis_index("x") * 8 + lax.axis_index("y") * 2 + lax.axis_index("zh")
    leaf = zl * 2 + core
    bits = [(core, "core", 1), (z0, "zl", 1), (z1, "zl", 2)]
    parts = [None, 64, 32]
    splits = [None, core, z0 * 2 + core]

    plans = []
    for t in range(3):
        slot = lax.dynamic_index_in_dim(slots[t], (leaf >> t) << t, 0, keepdims=False)
        present = slot >= 0
        at = jnp.maximum(slot, 0)
        plan = {}
        if t == 0:
            col, row, mine = at, at, present
        else:
            blk, pos = at // UPD, at % UPD + PIV
            part, r = parts[t], splits[t]
            col = blk * BLOCK + pos
            mine = present & (pos // part == r)
            row = jnp.where(mine, blk * part + pos - part * r, 0)
            far = jnp.where(mine, blk * (part + PIV) + pos - part * r, 0)
            plan["sel"] = part_of(far, front, BLOCK, 0)
            plan["far"] = far.reshape(NF, BLOCK)[:, :PIV].reshape(NP)
            plan["sel_mask"] = part_of(mine, front, BLOCK, 0).astype(F32)[:, None]
        plan["col"] = col
        plan["col_mask"] = present.astype(F32).reshape(NF, BLOCK)
        plan["row"] = row
        plan["row_mask"] = mine.astype(F32).reshape(NF, BLOCK)
        plan["piv"] = row.reshape(NF, BLOCK)[:, :PIV].reshape(NP)
        plan["piv_mask"] = plan["row_mask"][:, :PIV].reshape(NP // BLOCK, BLOCK)
        plan["ep"] = entries[t, 0].reshape(BLOCK, NF, BLOCK)[:, :, :PIV].reshape(BLOCK, NP)
        plans.append(plan)
    here, there = core.reshape(1), (1 - core).reshape(1)

    def placed(t, which, y):
        return recv(t, which, plans[t]["row"], plans[t]["row_mask"], y, entries)

    def summed(x, steps):
        for bit, axis, d in steps:
            x = x + swap(x, axis, d)
        return x

    def halved(x, step):
        bit, axis, d = step
        half = x.shape[1] // 2
        return part_of(x, bit, half, 1) + swap(part_of(x, 1 - bit, half, 1), axis, d)

    out = send(plans[0]["col"], plans[0]["col_mask"], child_update[0])
    y = lax.all_to_all(out, FRONT, split_axis=0, concat_axis=0, tiled=True).reshape(-1, BLOCK)
    y, plans = tie(y, plans)
    p, _ = panel(plans[0]["piv"], plans[0]["piv_mask"], y, plans[0]["ep"])
    p = summed(p, bits[:1])
    y, p = tie(y, p)
    away = placed(0, there, y)
    out = both_halves(jnp.concatenate([part_of(p, core, 64, 0), p[:PIV]], 0))
    y, out = tie(y, out)
    A = placed(0, here, y) + swap(away, "core", 1)
    got0 = gather_xy(out)
    mine = part_of(A, core, 64, 0)
    src = jnp.concatenate(ordered(core, mine, swap(part_of(A, 1 - core, 64, 0), "core", 1)), 1)
    out, got0 = tie(send(plans[1]["col"], plans[1]["col_mask"], src), got0)

    y = lax.all_to_all(out, FRONT, split_axis=0, concat_axis=0, tiled=True).reshape(-1, BLOCK)
    inv0 = inverse(got0)
    m0 = dot(p, inv0)
    sel = jnp.take(got0.reshape(-1, NP), plans[1]["sel"], axis=0) * plans[1]["sel_mask"]
    child = (got0, summed(sel, bits[:1]), inv0)
    flat = (plans[1]["far"], got0.reshape(-1, NP)) + child[1:]
    p, _ = panel(plans[1]["piv"], plans[1]["piv_mask"], y, plans[1]["ep"], flat)
    p = summed(p, bits[:1])
    y, p = tie(y, p)
    y = correct(64, y, *child)
    p = summed(p, bits[1:2])
    away = placed(1, there, y)
    y, p = tie(y, p)
    part = splits[2]
    out = both_halves(jnp.concatenate([part_of(p, part, 32, 0), p[:PIV]], 0))
    A = placed(1, here, y) + swap(away, "core", 1)
    A, out = tie(A, out)
    A = halved(A, bits[1])
    got1 = gather_xy(out)
    mine = part_of(A, z0, 64, 0)
    wide = ordered(z0, mine, swap(part_of(A, 1 - z0, 64, 0), "zl", 1))
    wide = jnp.concatenate(wide, 1)
    wide, got1 = tie(wide, got1)
    mine = part_of(wide, core, 32, 0)
    lo, hi = ordered(core, mine, swap(part_of(wide, 1 - core, 32, 0), "core", 1))
    w = F // 4
    src = jnp.concatenate([lo[:, :w], hi[:, :w], lo[:, w:], hi[:, w:]], 1)
    out = send(plans[2]["col"], plans[2]["col_mask"], src)

    y = lax.all_to_all(out, FRONT, split_axis=0, concat_axis=0, tiled=True).reshape(-1, BLOCK)
    inv1 = inverse(got1)
    m1 = dot(p, inv1)
    sel = jnp.take(got1.reshape(-1, NP), plans[2]["sel"], axis=0) * plans[2]["sel_mask"]
    child = (got1, summed(sel, bits[:2]), inv1)
    flat = (plans[2]["far"], got1.reshape(-1, NP)) + child[1:]
    p, q = panel(plans[2]["piv"], plans[2]["piv_mask"], y, plans[2]["ep"], flat)
    q = summed(q, bits[:1])
    y, q = tie(y, q)
    y = correct(32, y, *child)
    q = summed(q, bits[1:2])
    away = placed(2, there, y)
    y, q = tie(y, q)
    q = summed(q, bits[2:])
    A = placed(2, here, y)
    A, q = tie(A, q)
    gq = gather_all(q)
    rows = A[:PIV] + swap(away[:PIV], "core", 1)
    A = A + swap(away, "core", 1)
    rows = halved(rows, bits[1])
    A, rows = tie(A, rows)
    A = halved(A, bits[1])
    rows = halved(rows, bits[2])
    out = both_halves(rows)
    A, gq, out = lax.optimization_barrier((A, gq, out))
    p, gq = tie(p, gq)
    a12 = gather_xy(out)
    inv2 = inverse(gq)
    A = halved(A, bits[2])
    A, inv2 = tie(A, inv2)
    p = summed(p, bits)
    mult, top = last(A, a12, p, inv2, m0, m1)
    return mult[None], top


def solution(mesh):
    fine = Mesh(mesh.devices.reshape(4, 2, 4, 4, 2), LEAF + FRONT)
    in_specs = (P(LEAF, FRONT, None), P(None, LEAF, FRONT, None), P())
    out_specs = (P(LEAF, None, FRONT, None), P(FRONT, LEAF))
    return jax.shard_map(shards, mesh=fine, in_specs=in_specs, out_specs=out_specs, check_vma=False)
```

```python
import functools

import jax
import jax.numpy as jnp
from jax import lax
from jax.experimental import pallas as pl
from jax.experimental.pallas import tpu as pltpu
from jax.sharding import Mesh, PartitionSpec as P

F32 = jnp.float32
HIGHEST = lax.Precision.HIGHEST
BLOCK = 128
PIV = 8
UPD = BLOCK - PIV
NF = 32
F = NF * BLOCK
NP = NF * PIV
PER = 4
UNIT = PER * BLOCK
VMEM_LIMIT = 48 << 20
LEAF = ("zl", "core")
FRONT = ("x", "y", "zh")


def vmem():
    return pl.BlockSpec(memory_space=pltpu.VMEM)


def smem():
    return pl.BlockSpec(memory_space=pltpu.SMEM)


def params():
    return pltpu.CompilerParams(vmem_limit_bytes=VMEM_LIMIT)


def cost(us):
    return pl.CostEstimate(flops=0, bytes_accessed=int(us * 3.6e6), transcendentals=0)


def dot(a, b):
    return jnp.dot(a, b, precision=HIGHEST, preferred_element_type=F32)


def send_kernel(rows, pieces, terms, idx_ref, mask_ref, *refs):
    src, (out_ref, t_ref, g_ref) = refs[:-3], refs[-3:]
    step = pl.program_id(0)

    @pl.when(step == 0)
    def _():
        at = 0
        for p in range(pieces):
            for b in range(src[p * terms].shape[1] // BLOCK):
                blk = src[p * terms][:, b * BLOCK:(b + 1) * BLOCK]
                for j in range(1, terms):
                    blk = blk + src[p * terms + j][:, b * BLOCK:(b + 1) * BLOCK]
                if rows < BLOCK:
                    blk = jnp.concatenate([blk, jnp.zeros((BLOCK - rows, BLOCK), F32)], 0)
                t_ref[at:at + BLOCK, :] = blk.T
                at += BLOCK

    for j in range(PER):
        base = (step * PER + j) * BLOCK
        for k in range(BLOCK):
            g_ref[k:k + 1, :] = t_ref[pl.ds(idx_ref[base + k], 1), :]
        here = mask_ref[pl.ds(step * PER + j, 1), :]
        out_ref[j] = jnp.where(here > 0, g_ref[...].T[:rows], 0.0)


def send(idx, mask, *src):
    flat = [x for piece in src for x in piece]
    rows = flat[0].shape[0]
    cols = sum(piece[0].shape[1] for piece in src)
    return pl.pallas_call(
        functools.partial(send_kernel, rows, len(src), len(src[0])),
        grid=(NF // PER,),
        out_shape=jax.ShapeDtypeStruct((NF, rows, BLOCK), F32),
        in_specs=[smem()] + [vmem()] * (1 + len(flat)),
        out_specs=pl.BlockSpec((PER, rows, BLOCK), lambda i: (i, 0, 0)),
        scratch_shapes=[pltpu.VMEM((cols, BLOCK), F32), pltpu.VMEM((BLOCK, BLOCK), F32)],
        compiler_params=params(),
        cost_estimate=cost(7),
        name="send",
    )(idx, mask, *flat)


def place_pivots(idx_ref, y_ref, g_ref):
    for k in range(NP):
        g_ref[k:k + 1, :] = y_ref[pl.ds(idx_ref[k], 1), :]


def store_pivots(rows, mask_ref, ep_ref, p_ref, q_ref):
    for j in range(NP // BLOCK):
        c = slice(j * BLOCK, (j + 1) * BLOCK)
        blk = jnp.where(mask_ref[j:j + 1, :] > 0, rows[c].T, 0.0) + ep_ref[:, c]
        p_ref[:, c] = blk
        q_ref[:, c] = blk[:PIV]


def panel_kernel(idx_ref, mask_ref, y_ref, ep_ref, p_ref, q_ref, g_ref):
    place_pivots(idx_ref, y_ref, g_ref)
    store_pivots(g_ref[...], mask_ref, ep_ref, p_ref, q_ref)


def panel_less_kernel(idx_ref, mask_ref, y_ref, ep_ref, jdx_ref, got_ref, sel_ref, inv_ref, p_ref, q_ref, g_ref, h_ref):
    place_pivots(idx_ref, y_ref, g_ref)
    place_pivots(jdx_ref, got_ref, h_ref)
    rows = g_ref[...] - dot(h_ref[...], dot(sel_ref[...], inv_ref[...]).T)
    store_pivots(rows, mask_ref, ep_ref, p_ref, q_ref)


def panel(idx, mask, y, ep, child=()):
    return pl.pallas_call(
        panel_less_kernel if child else panel_kernel,
        out_shape=[jax.ShapeDtypeStruct((BLOCK, NP), F32), jax.ShapeDtypeStruct((PIV, NP), F32)],
        in_specs=[smem()] + [vmem()] * 3 + ([smem()] + [vmem()] * 3 if child else []),
        out_specs=[vmem(), vmem()],
        scratch_shapes=[pltpu.VMEM((NP, BLOCK), F32)] + [pltpu.VMEM((NP, NP), F32)] * (1 if child else 0),
        compiler_params=params(),
        cost_estimate=cost(3),
        name="panel",
    )(idx, mask, y, ep, *child)


def correct_kernel(part, y_ref, got_ref, sel_ref, inv_ref, yc_ref, m_ref):
    @pl.when(pl.program_id(0) == 0)
    def _():
        m_ref[...] = dot(sel_ref[...], inv_ref[...]).T

    got = got_ref[:, :part, :].reshape(-1, NP)
    yc_ref[...] = y_ref[...] - dot(got, m_ref[...])


def correct(part, y, got, sel, inv):
    rows = y.shape[0] // 4
    return pl.pallas_call(
        functools.partial(correct_kernel, part),
        grid=(4,),
        out_shape=jax.ShapeDtypeStruct(y.shape, F32),
        in_specs=[
            pl.BlockSpec((rows, BLOCK), lambda i: (i, 0)),
            pl.BlockSpec((NF // 4, part + PIV, NP), lambda i: (i, 0, 0)),
            vmem(),
            vmem(),
        ],
        out_specs=pl.BlockSpec((rows, BLOCK), lambda i: (i, 0)),
        scratch_shapes=[pltpu.VMEM((NP, BLOCK), F32)],
        compiler_params=params(),
        cost_estimate=cost(4),
        name="correct",
    )(y, got, sel, inv)


def recv_kernel(split, unit_ref, core_ref, idx_ref, mask_ref, y_ref, e_ref, *refs):
    g_ref = refs[-1]
    unit = unit_ref[pl.program_id(0)]
    for j in range(PER):
        base = (unit * PER + j) * BLOCK
        for k in range(BLOCK):
            g_ref[k:k + 1, :] = y_ref[pl.ds(idx_ref[base + k], 1), :]
        here = mask_ref[pl.ds(unit * PER + j, 1), :]
        c = slice(j * BLOCK, (j + 1) * BLOCK)
        blk = jnp.where(here > 0, g_ref[...].T, 0.0) + e_ref[0, 0, :, c]
        if split:
            lo, hi = blk[:BLOCK // 2], blk[BLOCK // 2:]
            first = core_ref[0] == 0
            refs[0][:, c] = jnp.where(first, hi, lo)
            refs[1][:, c] = jnp.where(first, lo, hi)
        else:
            refs[0][:, c] = blk


def recv(level, split, units, core, idx, mask, y, entries):
    n = units.shape[0]
    rows = BLOCK // 2 if split else BLOCK
    outs = 2 if split else 1
    return pl.pallas_call(
        functools.partial(recv_kernel, split),
        grid_spec=pltpu.PrefetchScalarGridSpec(
            num_scalar_prefetch=3,
            grid=(n,),
            in_specs=[
                vmem(),
                vmem(),
                pl.BlockSpec((1, 1, BLOCK, UNIT), lambda i, u, c, s: (level, 0, 0, u[i])),
            ],
            out_specs=[pl.BlockSpec((rows, UNIT), lambda i, u, c, s: (0, i))] * outs,
            scratch_shapes=[pltpu.VMEM((BLOCK, BLOCK), F32)],
        ),
        out_shape=[jax.ShapeDtypeStruct((rows, n * UNIT), F32)] * outs,
        compiler_params=params(),
        cost_estimate=cost(1.15 * n),
        name="recv",
    )(units, core, idx, mask, y, entries)


def inv_small(D, n, step):
    rows = lax.broadcasted_iota(jnp.int32, (n, n), 0)
    cols = lax.broadcasted_iota(jnp.int32, (n, n), 1)
    lane = lax.broadcasted_iota(jnp.int32, (1, n), 1)
    for k in range(0, n, step):
        C = [jnp.broadcast_to(D[:, k + j:k + j + 1], (n, n)) for j in range(step)]
        B = [[C[j][k + i:k + i + 1, :] for j in range(step)] for i in range(step)]
        R = []
        for i in range(step):
            unit = jnp.where(lane == k + i, 1.0, 0.0)
            R.append(jnp.where((lane >= k) & (lane < k + step), unit, D[k + i:k + i + 1, :]))
        for p in range(step):
            d = 1.0 / B[p][p]
            for j in range(p + 1, step):
                B[p][j] = B[p][j] * d
            R[p] = R[p] * d
            for i in range(step):
                if i != p:
                    f = B[i][p]
                    for j in range(p + 1, step):
                        B[i][j] = B[i][j] - f * B[p][j]
                    R[i] = R[i] - f * R[p]
        D = jnp.where((cols >= k) & (cols < k + step), 0.0, D)
        for j in range(step):
            D = D - C[j] * R[j]
        for i in range(step):
            D = jnp.where(rows == k + i, R[i], D)
    return D


def inv_kernel(nb, a_ref, o_ref):
    o_ref[...] = a_ref[...].reshape(NP, NP)
    for b in range(NP // nb):
        lo = b * nb
        Ab = o_ref[:, lo:lo + nb]
        Dinv = inv_small(Ab[lo:lo + nb, :], nb, 8)
        lane = lax.broadcasted_iota(jnp.int32, (nb, NP), 1)
        eye = (lane - lo == lax.broadcasted_iota(jnp.int32, (nb, NP), 0)).astype(F32)
        Rb = jnp.where((lane >= lo) & (lane < lo + nb), eye, o_ref[lo:lo + nb, :])
        Rn = dot(Dinv, Rb)
        lane2 = lax.broadcasted_iota(jnp.int32, (NP, NP), 1)
        rest = jnp.where((lane2 >= lo) & (lane2 < lo + nb), 0.0, o_ref[...])
        o_ref[...] = rest - dot(Ab, Rn)
        o_ref[lo:lo + nb, :] = Rn


def inverse(got):
    last = got.shape[1] // PIV - 1
    return pl.pallas_call(
        functools.partial(inv_kernel, 64),
        grid=(1,),
        out_shape=jax.ShapeDtypeStruct((NP, NP), F32),
        in_specs=[pl.BlockSpec((NF, PIV, NP), lambda i: (0, last, 0))],
        out_specs=pl.BlockSpec((NP, NP), lambda i: (0, 0)),
        compiler_params=params(),
        cost_estimate=cost(12),
        name="inverse",
    )(got)


def last_kernel(a_ref, a12_ref, p_ref, inv_ref, m0_ref, m1_ref, mult_ref, top_ref):
    m = dot(p_ref[...], inv_ref[...])
    mult_ref[0] = m0_ref[PIV:, :]
    mult_ref[1] = m1_ref[PIV:, :]
    mult_ref[2] = m[PIV:, :]
    a12 = a12_ref[...].reshape(NP, UNIT)
    s = a_ref[...] - dot(m, a12)
    for j in range(PER):
        top_ref[:, j * UPD:(j + 1) * UPD] = s[PIV:, j * BLOCK + PIV:(j + 1) * BLOCK]


def last(a, a12, p, inv, m0, m1):
    return pl.pallas_call(
        last_kernel,
        out_shape=[jax.ShapeDtypeStruct((3, UPD, NP), F32), jax.ShapeDtypeStruct((UPD, PER * UPD), F32)],
        in_specs=[vmem()] * 6,
        out_specs=[vmem(), vmem()],
        compiler_params=params(),
        cost_estimate=cost(2),
        name="last",
    )(a, a12, p, inv, m0, m1)


def swap(x, axis, d):
    n = lax.axis_size(axis)
    return lax.ppermute(x, axis, [(i, i ^ d) for i in range(n)])


def part_of(x, i, size, dim):
    return lax.dynamic_slice_in_dim(x, i * size, size, dim)


def ordered(bit, mine, other):
    return jnp.where(bit == 0, mine, other), jnp.where(bit == 0, other, mine)


def tie(x, y):
    return lax.optimization_barrier((x, y))


def both_halves(x):
    both = jnp.stack(ordered(lax.axis_index("zh"), x, swap(x, "zh", 1)))
    return jnp.broadcast_to(both[None], (NF // 2,) + both.shape)


def gather_xy(out):
    got = lax.all_to_all(out, ("x", "y"), split_axis=0, concat_axis=0, tiled=True)
    return got.reshape((NF,) + out.shape[2:])


def gather_all(x):
    out = jnp.broadcast_to(x[None], (NF,) + x.shape)
    return lax.all_to_all(out, FRONT, split_axis=0, concat_axis=0, tiled=True)


def shards(child_update, entries, slots):
    zl = lax.axis_index("zl")
    core = lax.axis_index("core")
    z0, z1 = zl & 1, zl >> 1
    front = lax.axis_index("x") * 8 + lax.axis_index("y") * 2 + lax.axis_index("zh")
    leaf = zl * 2 + core
    bits = [(core, "core", 1), (z0, "zl", 1), (z1, "zl", 2)]
    parts = [None, 64, 32]
    splits = [None, core, core * 2 + z0]

    plans = []
    for t in range(3):
        slot = lax.dynamic_index_in_dim(slots[t], (leaf >> t) << t, 0, keepdims=False)
        present = slot >= 0
        at = jnp.maximum(slot, 0)
        plan = {}
        if t == 0:
            col, row, mine = at, at, present
        else:
            blk, pos = at // UPD, at % UPD + PIV
            part, r = parts[t], splits[t]
            col = blk * BLOCK + pos
            mine = present & (pos // part == r)
            row = jnp.where(mine, blk * part + pos - part * r, 0)
            far = jnp.where(mine, blk * (part + PIV) + pos - part * r, 0)
            plan["sel"] = part_of(far, front, BLOCK, 0)
            plan["far"] = far.reshape(NF, BLOCK)[:, :PIV].reshape(NP)
            plan["sel_mask"] = part_of(mine, front, BLOCK, 0).astype(F32)[:, None]
        plan["col"] = col
        plan["col_mask"] = present.astype(F32).reshape(NF, BLOCK)
        plan["row"] = row
        plan["row_mask"] = mine.astype(F32).reshape(NF, BLOCK)
        plan["piv"] = row.reshape(NF, BLOCK)[:, :PIV].reshape(NP)
        plan["piv_mask"] = plan["row_mask"][:, :PIV].reshape(NP // BLOCK, BLOCK)
        plan["ep"] = entries[t, 0].reshape(BLOCK, NF, BLOCK)[:, :, :PIV].reshape(BLOCK, NP)
        plans.append(plan)
    whose = core.reshape(1)
    halves = [jnp.arange(4, dtype=jnp.int32) + 4 * h for h in range(2)]
    quads = [jnp.arange(2, dtype=jnp.int32) * 4 + z * 2 + c for z, c in ((1 - z0, 1 - core), (1 - z0, core), (z0, 1 - core), (z0, core))]
    plans, whose, halves, quads = lax.optimization_barrier((plans, whose, halves, quads))

    def placed(t, split, units, y):
        return recv(t, split, units, whose, plans[t]["row"], plans[t]["row_mask"], y, entries)

    def summed(x, steps):
        for bit, axis, d in steps:
            x = x + swap(x, axis, d)
        return x

    def exchange(out):
        return lax.all_to_all(out, FRONT, split_axis=0, concat_axis=0, tiled=True).reshape(-1, BLOCK)

    y = exchange(send(plans[0]["col"], plans[0]["col_mask"], (child_update[0],)))
    y, plans = tie(y, plans)
    p, _ = panel(plans[0]["piv"], plans[0]["piv_mask"], y, plans[0]["ep"])
    p = summed(p, bits[:1])
    out = both_halves(jnp.concatenate([part_of(p, core, 64, 0), p[:PIV]], 0))
    y, out = tie(y, out)
    got0 = gather_xy(out)
    src = []
    for h in halves:
        away, keep = placed(0, True, h, y)
        src.append((keep, swap(away, "core", 1)))
    out, got0 = tie(send(plans[1]["col"], plans[1]["col_mask"], *src), got0)

    y = exchange(out)
    inv0 = inverse(got0)
    m0 = dot(p, inv0)
    sel = jnp.take(got0.reshape(-1, NP), plans[1]["sel"], axis=0) * plans[1]["sel_mask"]
    child = (got0, summed(sel, bits[:1]), inv0)
    flat = (plans[1]["far"], got0.reshape(-1, NP)) + child[1:]
    p, _ = panel(plans[1]["piv"], plans[1]["piv_mask"], y, plans[1]["ep"], flat)
    p = summed(p, bits[:1])
    y = correct(64, y, *child)
    y, p = tie(y, p)
    p = summed(p, bits[1:2])
    src = []
    for h in halves:
        away, keep = placed(1, True, h, y)
        if not src:
            y, p = tie(y, p)
            out = both_halves(jnp.concatenate([part_of(p, splits[2], 32, 0), p[:PIV]], 0))
        rows = keep + swap(away, "core", 1)
        src.append((part_of(rows, z0, 32, 0), swap(part_of(rows, 1 - z0, 32, 0), "zl", 1)))
    got1 = gather_xy(out)
    out, got1 = tie(send(plans[2]["col"], plans[2]["col_mask"], *src), got1)

    y = exchange(out)
    inv1 = inverse(got1)
    m1 = dot(p, inv1)
    sel = jnp.take(got1.reshape(-1, NP), plans[2]["sel"], axis=0) * plans[2]["sel_mask"]
    child = (got1, summed(sel, bits[:2]), inv1)
    flat = (plans[2]["far"], got1.reshape(-1, NP)) + child[1:]
    p, q = panel(plans[2]["piv"], plans[2]["piv_mask"], y, plans[2]["ep"], flat)
    q = summed(q, bits)
    y = correct(32, y, *child)
    y, q = tie(y, q)
    gq = gather_all(q)
    a = [placed(2, False, u, y)[0] for u in quads[:2]]
    far = a[1] + swap(a[0], "core", 1)
    rows = swap(far[:PIV], "zl", 1)
    far, rows = tie(far, rows)
    far = swap(far, "zl", 1)
    a = [placed(2, False, u, y)[0] for u in quads[2:]]
    near = a[1] + swap(a[0], "core", 1)
    rows = rows + near[:PIV]
    w = rows.shape[1] // 2
    rows = part_of(rows, z1, w, 1) + swap(part_of(rows, 1 - z1, w, 1), "zl", 2)
    out = both_halves(rows)
    p = summed(p, bits)
    out, p, gq = lax.optimization_barrier((out, p, gq))
    a12 = gather_xy(out)
    inv2 = inverse(gq)
    A = near + far
    A = part_of(A, z1, w, 1) + swap(part_of(A, 1 - z1, w, 1), "zl", 2)
    mult, top = last(A, a12, p, inv2, m0, m1)
    return mult[None], top


def solution(mesh):
    fine = Mesh(mesh.devices.reshape(4, 2, 4, 4, 2), LEAF + FRONT)
    in_specs = (P(LEAF, FRONT, None), P(None, LEAF, FRONT, None), P())
    out_specs = (P(LEAF, None, FRONT, None), P(FRONT, LEAF))
    return jax.shard_map(shards, mesh=fine, in_specs=in_specs, out_specs=out_specs, check_vma=False)
```

```python
import functools

import jax
import jax.numpy as jnp
from jax import lax
from jax.experimental import pallas as pl
from jax.experimental.pallas import tpu as pltpu
from jax.sharding import Mesh, PartitionSpec as P

F32 = jnp.float32
HIGHEST = lax.Precision.HIGHEST
BLOCK = 128
PIV = 8
UPD = BLOCK - PIV
NF = 32
F = NF * BLOCK
NP = NF * PIV
PER = 4
UNIT = PER * BLOCK
VMEM_LIMIT = 20 << 20
LEAF = ("zl", "core")
FRONT = ("x", "y", "zh")


def vmem():
    return pl.BlockSpec(memory_space=pltpu.VMEM)


def smem():
    return pl.BlockSpec(memory_space=pltpu.SMEM)


def params():
    return pltpu.CompilerParams(vmem_limit_bytes=VMEM_LIMIT)


def cost(us):
    return pl.CostEstimate(flops=0, bytes_accessed=int(us * 3.6e6), transcendentals=0)


def dot(a, b):
    return jnp.dot(a, b, precision=HIGHEST, preferred_element_type=F32)


def send_kernel(rows, pieces, terms, idx_ref, mask_ref, *refs):
    src, (out_ref, t_ref, g_ref) = refs[:-3], refs[-3:]
    step = pl.program_id(0)

    @pl.when(step == 0)
    def _():
        at = 0
        for p in range(pieces):
            for b in range(src[p * terms].shape[1] // BLOCK):
                blk = src[p * terms][:, b * BLOCK:(b + 1) * BLOCK]
                for j in range(1, terms):
                    blk = blk + src[p * terms + j][:, b * BLOCK:(b + 1) * BLOCK]
                if rows < BLOCK:
                    blk = jnp.concatenate([blk, jnp.zeros((BLOCK - rows, BLOCK), F32)], 0)
                t_ref[at:at + BLOCK, :] = blk.T
                at += BLOCK

    for j in range(PER):
        base = (step * PER + j) * BLOCK
        for k in range(BLOCK):
            g_ref[k:k + 1, :] = t_ref[pl.ds(idx_ref[base + k], 1), :]
        here = mask_ref[pl.ds(step * PER + j, 1), :]
        out_ref[j] = jnp.where(here > 0, g_ref[...].T[:rows], 0.0)


def send(idx, mask, *src):
    flat = [x for piece in src for x in piece]
    rows = flat[0].shape[0]
    cols = sum(piece[0].shape[1] for piece in src)
    return pl.pallas_call(
        functools.partial(send_kernel, rows, len(src), len(src[0])),
        grid=(NF // PER,),
        out_shape=jax.ShapeDtypeStruct((NF, rows, BLOCK), F32),
        in_specs=[smem()] + [vmem()] * (1 + len(flat)),
        out_specs=pl.BlockSpec((PER, rows, BLOCK), lambda i: (i, 0, 0)),
        scratch_shapes=[pltpu.VMEM((cols, BLOCK), F32), pltpu.VMEM((BLOCK, BLOCK), F32)],
        compiler_params=params(),
        cost_estimate=cost(7),
        name="send",
    )(idx, mask, *flat)


def place_pivots(idx_ref, y_ref, g_ref):
    for k in range(NP):
        g_ref[k:k + 1, :] = y_ref[pl.ds(idx_ref[k], 1), :]


def store_pivots(rows, mask_ref, ep_ref, p_ref, q_ref):
    for j in range(NP // BLOCK):
        c = slice(j * BLOCK, (j + 1) * BLOCK)
        blk = jnp.where(mask_ref[j:j + 1, :] > 0, rows[c].T, 0.0) + ep_ref[:, c]
        p_ref[:, c] = blk
        q_ref[:, c] = blk[:PIV]


def panel_kernel(idx_ref, mask_ref, y_ref, ep_ref, p_ref, q_ref, g_ref):
    place_pivots(idx_ref, y_ref, g_ref)
    store_pivots(g_ref[...], mask_ref, ep_ref, p_ref, q_ref)


def panel_less_kernel(idx_ref, mask_ref, y_ref, ep_ref, jdx_ref, got_ref, sel_ref, inv_ref, p_ref, q_ref, g_ref, h_ref):
    place_pivots(idx_ref, y_ref, g_ref)
    place_pivots(jdx_ref, got_ref, h_ref)
    rows = g_ref[...] - dot(h_ref[...], dot(sel_ref[...], inv_ref[...]).T)
    store_pivots(rows, mask_ref, ep_ref, p_ref, q_ref)


def panel(idx, mask, y, ep, child=()):
    return pl.pallas_call(
        panel_less_kernel if child else panel_kernel,
        out_shape=[jax.ShapeDtypeStruct((BLOCK, NP), F32), jax.ShapeDtypeStruct((PIV, NP), F32)],
        in_specs=[smem()] + [vmem()] * 3 + ([smem()] + [vmem()] * 3 if child else []),
        out_specs=[vmem(), vmem()],
        scratch_shapes=[pltpu.VMEM((NP, BLOCK), F32)] + [pltpu.VMEM((NP, NP), F32)] * (1 if child else 0),
        compiler_params=params(),
        cost_estimate=cost(3),
        name="panel",
    )(idx, mask, y, ep, *child)


def correct_kernel(part, y_ref, got_ref, sel_ref, inv_ref, yc_ref, m_ref):
    @pl.when(pl.program_id(0) == 0)
    def _():
        m_ref[...] = dot(sel_ref[...], inv_ref[...]).T

    got = got_ref[:, :part, :].reshape(-1, NP)
    yc_ref[...] = y_ref[...] - dot(got, m_ref[...])


def correct(part, y, got, sel, inv):
    rows = y.shape[0] // 4
    return pl.pallas_call(
        functools.partial(correct_kernel, part),
        grid=(4,),
        out_shape=jax.ShapeDtypeStruct(y.shape, F32),
        in_specs=[
            pl.BlockSpec((rows, BLOCK), lambda i: (i, 0)),
            pl.BlockSpec((NF // 4, part + PIV, NP), lambda i: (i, 0, 0)),
            vmem(),
            vmem(),
        ],
        out_specs=pl.BlockSpec((rows, BLOCK), lambda i: (i, 0)),
        scratch_shapes=[pltpu.VMEM((NP, BLOCK), F32)],
        compiler_params=params(),
        cost_estimate=cost(4),
        name="correct",
    )(y, got, sel, inv)


def recv_kernel(split, unit_ref, core_ref, idx_ref, mask_ref, y_ref, e_ref, *refs):
    g_ref = refs[-1]
    unit = unit_ref[pl.program_id(0)]
    for j in range(PER):
        base = (unit * PER + j) * BLOCK
        for k in range(BLOCK):
            g_ref[k:k + 1, :] = y_ref[pl.ds(idx_ref[base + k], 1), :]
        here = mask_ref[pl.ds(unit * PER + j, 1), :]
        c = slice(j * BLOCK, (j + 1) * BLOCK)
        blk = jnp.where(here > 0, g_ref[...].T, 0.0) + e_ref[0, 0, :, c]
        if split:
            lo, hi = blk[:BLOCK // 2], blk[BLOCK // 2:]
            first = core_ref[0] == 0
            refs[0][:, c] = jnp.where(first, hi, lo)
            refs[1][:, c] = jnp.where(first, lo, hi)
        else:
            refs[0][:, c] = blk


def recv(level, split, units, core, idx, mask, y, entries):
    n = units.shape[0]
    rows = BLOCK // 2 if split else BLOCK
    outs = 2 if split else 1
    return pl.pallas_call(
        functools.partial(recv_kernel, split),
        grid_spec=pltpu.PrefetchScalarGridSpec(
            num_scalar_prefetch=3,
            grid=(n,),
            in_specs=[
                vmem(),
                vmem(),
                pl.BlockSpec((1, 1, BLOCK, UNIT), lambda i, u, c, s: (level, 0, 0, u[i])),
            ],
            out_specs=[pl.BlockSpec((rows, UNIT), lambda i, u, c, s: (0, i))] * outs,
            scratch_shapes=[pltpu.VMEM((BLOCK, BLOCK), F32)],
        ),
        out_shape=[jax.ShapeDtypeStruct((rows, n * UNIT), F32)] * outs,
        compiler_params=params(),
        cost_estimate=cost(1.15 * n),
        name="recv",
    )(units, core, idx, mask, y, entries)


def inv_small(D, n, step):
    rows = lax.broadcasted_iota(jnp.int32, (n, n), 0)
    cols = lax.broadcasted_iota(jnp.int32, (n, n), 1)
    lane = lax.broadcasted_iota(jnp.int32, (1, n), 1)
    for k in range(0, n, step):
        C = [jnp.broadcast_to(D[:, k + j:k + j + 1], (n, n)) for j in range(step)]
        B = [[C[j][k + i:k + i + 1, :] for j in range(step)] for i in range(step)]
        R = []
        for i in range(step):
            unit = jnp.where(lane == k + i, 1.0, 0.0)
            R.append(jnp.where((lane >= k) & (lane < k + step), unit, D[k + i:k + i + 1, :]))
        for p in range(step):
            d = 1.0 / B[p][p]
            for j in range(p + 1, step):
                B[p][j] = B[p][j] * d
            R[p] = R[p] * d
            for i in range(step):
                if i != p:
                    f = B[i][p]
                    for j in range(p + 1, step):
                        B[i][j] = B[i][j] - f * B[p][j]
                    R[i] = R[i] - f * R[p]
        D = jnp.where((cols >= k) & (cols < k + step), 0.0, D)
        for j in range(step):
            D = D - C[j] * R[j]
        for i in range(step):
            D = jnp.where(rows == k + i, R[i], D)
    return D


def inv_kernel(nb, a_ref, o_ref):
    o_ref[...] = a_ref[...].reshape(NP, NP)
    for b in range(NP // nb):
        lo = b * nb
        Ab = o_ref[:, lo:lo + nb]
        Dinv = inv_small(Ab[lo:lo + nb, :], nb, 8)
        lane = lax.broadcasted_iota(jnp.int32, (nb, NP), 1)
        eye = (lane - lo == lax.broadcasted_iota(jnp.int32, (nb, NP), 0)).astype(F32)
        Rb = jnp.where((lane >= lo) & (lane < lo + nb), eye, o_ref[lo:lo + nb, :])
        Rn = dot(Dinv, Rb)
        lane2 = lax.broadcasted_iota(jnp.int32, (NP, NP), 1)
        rest = jnp.where((lane2 >= lo) & (lane2 < lo + nb), 0.0, o_ref[...])
        o_ref[...] = rest - dot(Ab, Rn)
        o_ref[lo:lo + nb, :] = Rn


def inverse(got):
    last = got.shape[1] // PIV - 1
    return pl.pallas_call(
        functools.partial(inv_kernel, 64),
        grid=(1,),
        out_shape=jax.ShapeDtypeStruct((NP, NP), F32),
        in_specs=[pl.BlockSpec((NF, PIV, NP), lambda i: (0, last, 0))],
        out_specs=pl.BlockSpec((NP, NP), lambda i: (0, 0)),
        compiler_params=params(),
        cost_estimate=cost(12),
        name="inverse",
    )(got)


def last_kernel(a_ref, a12_ref, p_ref, inv_ref, m0_ref, m1_ref, mult_ref, top_ref):
    m = dot(p_ref[...], inv_ref[...])
    mult_ref[0] = m0_ref[PIV:, :]
    mult_ref[1] = m1_ref[PIV:, :]
    mult_ref[2] = m[PIV:, :]
    a12 = a12_ref[...].reshape(NP, UNIT)
    s = a_ref[...] - dot(m, a12)
    for j in range(PER):
        top_ref[:, j * UPD:(j + 1) * UPD] = s[PIV:, j * BLOCK + PIV:(j + 1) * BLOCK]


def last(a, a12, p, inv, m0, m1):
    return pl.pallas_call(
        last_kernel,
        out_shape=[jax.ShapeDtypeStruct((3, UPD, NP), F32), jax.ShapeDtypeStruct((UPD, PER * UPD), F32)],
        in_specs=[vmem()] * 6,
        out_specs=[vmem(), vmem()],
        compiler_params=params(),
        cost_estimate=cost(2),
        name="last",
    )(a, a12, p, inv, m0, m1)


def swap(x, axis, d):
    n = lax.axis_size(axis)
    return lax.ppermute(x, axis, [(i, i ^ d) for i in range(n)])


def part_of(x, i, size, dim):
    return lax.dynamic_slice_in_dim(x, i * size, size, dim)


def ordered(bit, mine, other):
    return jnp.where(bit == 0, mine, other), jnp.where(bit == 0, other, mine)


def tie(x, y):
    return lax.optimization_barrier((x, y))


def both_halves(x):
    both = jnp.stack(ordered(lax.axis_index("zh"), x, swap(x, "zh", 1)))
    return jnp.broadcast_to(both[None], (NF // 2,) + both.shape)


def gather_xy(out):
    got = lax.all_to_all(out, ("x", "y"), split_axis=0, concat_axis=0, tiled=True)
    return got.reshape((NF,) + out.shape[2:])


def gather_all(x):
    out = jnp.broadcast_to(x[None], (NF,) + x.shape)
    return lax.all_to_all(out, FRONT, split_axis=0, concat_axis=0, tiled=True)


def shards(child_update, entries, slots):
    zl = lax.axis_index("zl")
    core = lax.axis_index("core")
    z0, z1 = zl & 1, zl >> 1
    front = lax.axis_index("x") * 8 + lax.axis_index("y") * 2 + lax.axis_index("zh")
    leaf = zl * 2 + core
    bits = [(core, "core", 1), (z0, "zl", 1), (z1, "zl", 2)]
    parts = [None, 64, 32]
    splits = [None, core, core * 2 + z0]

    plans = []
    for t in range(3):
        slot = lax.dynamic_index_in_dim(slots[t], (leaf >> t) << t, 0, keepdims=False)
        present = slot >= 0
        at = jnp.maximum(slot, 0)
        plan = {}
        if t == 0:
            col, row, mine = at, at, present
        else:
            blk, pos = at // UPD, at % UPD + PIV
            part, r = parts[t], splits[t]
            col = blk * BLOCK + pos
            mine = present & (pos // part == r)
            row = jnp.where(mine, blk * part + pos - part * r, 0)
            far = jnp.where(mine, blk * (part + PIV) + pos - part * r, 0)
            plan["sel"] = part_of(far, front, BLOCK, 0)
            plan["far"] = far.reshape(NF, BLOCK)[:, :PIV].reshape(NP)
            plan["sel_mask"] = part_of(mine, front, BLOCK, 0).astype(F32)[:, None]
        plan["col"] = col
        plan["col_mask"] = present.astype(F32).reshape(NF, BLOCK)
        plan["row"] = row
        plan["row_mask"] = mine.astype(F32).reshape(NF, BLOCK)
        plan["piv"] = row.reshape(NF, BLOCK)[:, :PIV].reshape(NP)
        plan["piv_mask"] = plan["row_mask"][:, :PIV].reshape(NP // BLOCK, BLOCK)
        plan["ep"] = entries[t, 0].reshape(BLOCK, NF, BLOCK)[:, :, :PIV].reshape(BLOCK, NP)
        plans.append(plan)
    whose = core.reshape(1)
    halves = [jnp.arange(4, dtype=jnp.int32) + 4 * h for h in range(2)]
    quads = [jnp.arange(2, dtype=jnp.int32) * 4 + z * 2 + c for z, c in ((1 - z0, 1 - core), (1 - z0, core), (z0, 1 - core), (z0, core))]

    def placed(t, split, units, y):
        return recv(t, split, units, whose, plans[t]["row"], plans[t]["row_mask"], y, entries)

    def summed(x, steps):
        for bit, axis, d in steps:
            x = x + swap(x, axis, d)
        return x

    def exchange(out):
        return lax.all_to_all(out, FRONT, split_axis=0, concat_axis=0, tiled=True).reshape(-1, BLOCK)

    y = exchange(send(plans[0]["col"], plans[0]["col_mask"], (child_update[0],)))
    y, plans = tie(y, plans)
    p, _ = panel(plans[0]["piv"], plans[0]["piv_mask"], y, plans[0]["ep"])
    p = summed(p, bits[:1])
    out = both_halves(jnp.concatenate([part_of(p, core, 64, 0), p[:PIV]], 0))
    y, out = tie(y, out)
    got0 = gather_xy(out)
    src = []
    for h in halves:
        away, keep = placed(0, True, h, y)
        src.append((keep, swap(away, "core", 1)))
    out, got0 = tie(send(plans[1]["col"], plans[1]["col_mask"], *src), got0)

    y = exchange(out)
    inv0 = inverse(got0)
    m0 = dot(p, inv0)
    sel = jnp.take(got0.reshape(-1, NP), plans[1]["sel"], axis=0) * plans[1]["sel_mask"]
    child = (got0, summed(sel, bits[:1]), inv0)
    flat = (plans[1]["far"], got0.reshape(-1, NP)) + child[1:]
    p, _ = panel(plans[1]["piv"], plans[1]["piv_mask"], y, plans[1]["ep"], flat)
    p = summed(p, bits[:1])
    y = correct(64, y, *child)
    y, p = tie(y, p)
    p = summed(p, bits[1:2])
    away, keep = placed(1, True, halves[0], y)
    p, away, keep = lax.optimization_barrier((p, away, keep))
    out = both_halves(jnp.concatenate([part_of(p, splits[2], 32, 0), p[:PIV]], 0))
    out, second = tie(out, placed(1, True, halves[1], y)[::-1])
    src = [(keep, away), second]
    got1 = gather_xy(out)
    for h in range(2):
        rows = src[h][0] + swap(src[h][1], "core", 1)
        src[h] = part_of(rows, z0, 32, 0), swap(part_of(rows, 1 - z0, 32, 0), "zl", 1)
    out, got1 = tie(send(plans[2]["col"], plans[2]["col_mask"], *src), got1)

    y = exchange(out)
    inv1 = inverse(got1)
    m1 = dot(p, inv1)
    sel = jnp.take(got1.reshape(-1, NP), plans[2]["sel"], axis=0) * plans[2]["sel_mask"]
    child = (got1, summed(sel, bits[:2]), inv1)
    flat = (plans[2]["far"], got1.reshape(-1, NP)) + child[1:]
    p, q = panel(plans[2]["piv"], plans[2]["piv_mask"], y, plans[2]["ep"], flat)
    q = summed(q, bits)
    y = correct(32, y, *child)
    y, q = tie(y, q)
    gq = gather_all(q)
    a = [placed(2, False, u, y)[0] for u in quads]
    far = a[1] + swap(a[0], "core", 1)
    near = a[3] + swap(a[2], "core", 1)
    p = summed(p, bits)
    rows = near[:PIV] + swap(far[:PIV], "zl", 1)
    far, rows, near, p, gq = lax.optimization_barrier((far, rows, near, p, gq))
    far = swap(far, "zl", 1)
    w = far.shape[1] // 2
    rows = part_of(rows, z1, w, 1) + swap(part_of(rows, 1 - z1, w, 1), "zl", 2)
    out = both_halves(rows)
    A, out = tie(near + far, out)
    a12 = gather_xy(out)
    inv2 = inverse(gq)
    A = part_of(A, z1, w, 1) + swap(part_of(A, 1 - z1, w, 1), "zl", 2)
    mult, top = last(A, a12, p, inv2, m0, m1)
    return mult[None], top


def solution(mesh):
    fine = Mesh(mesh.devices.reshape(4, 2, 4, 4, 2), LEAF + FRONT)
    in_specs = (P(LEAF, FRONT, None), P(None, LEAF, FRONT, None), P())
    out_specs = (P(LEAF, None, FRONT, None), P(FRONT, LEAF))
    return jax.shard_map(shards, mesh=fine, in_specs=in_specs, out_specs=out_specs, check_vma=False)
```

```python
import functools

import jax
import jax.numpy as jnp
from jax import lax
from jax.experimental import pallas as pl
from jax.experimental.pallas import tpu as pltpu
from jax.sharding import Mesh, PartitionSpec as P

F32 = jnp.float32
HIGHEST = lax.Precision.HIGHEST
BLOCK = 128
PIV = 8
UPD = BLOCK - PIV
NF = 32
F = NF * BLOCK
NP = NF * PIV
PER = 4
UNIT = PER * BLOCK
VMEM_LIMIT = 20 << 20
LEAF = ("zl", "core")
FRONT = ("x", "y", "zh")


def vmem():
    return pl.BlockSpec(memory_space=pltpu.VMEM)


def smem():
    return pl.BlockSpec(memory_space=pltpu.SMEM)


def params():
    return pltpu.CompilerParams(vmem_limit_bytes=VMEM_LIMIT)


def cost(us):
    return pl.CostEstimate(flops=0, bytes_accessed=int(us * 3.6e6), transcendentals=0)


def dot(a, b):
    return jnp.dot(a, b, precision=HIGHEST, preferred_element_type=F32)


def send_kernel(rows, pieces, terms, idx_ref, mask_ref, *refs):
    src, (out_ref, t_ref, g_ref) = refs[:-3], refs[-3:]
    step = pl.program_id(0)

    @pl.when(step == 0)
    def _():
        at = 0
        for p in range(pieces):
            for b in range(src[p * terms].shape[1] // BLOCK):
                blk = src[p * terms][:, b * BLOCK:(b + 1) * BLOCK]
                for j in range(1, terms):
                    blk = blk + src[p * terms + j][:, b * BLOCK:(b + 1) * BLOCK]
                if rows < BLOCK:
                    blk = jnp.concatenate([blk, jnp.zeros((BLOCK - rows, BLOCK), F32)], 0)
                t_ref[at:at + BLOCK, :] = blk.T
                at += BLOCK

    for j in range(PER):
        base = (step * PER + j) * BLOCK
        for k in range(BLOCK):
            g_ref[k:k + 1, :] = t_ref[pl.ds(idx_ref[base + k], 1), :]
        here = mask_ref[pl.ds(step * PER + j, 1), :]
        out_ref[j] = jnp.where(here > 0, g_ref[...].T[:rows], 0.0)


def send(idx, mask, *src):
    flat = [x for piece in src for x in piece]
    rows = flat[0].shape[0]
    cols = sum(piece[0].shape[1] for piece in src)
    return pl.pallas_call(
        functools.partial(send_kernel, rows, len(src), len(src[0])),
        grid=(NF // PER,),
        out_shape=jax.ShapeDtypeStruct((NF, rows, BLOCK), F32),
        in_specs=[smem()] + [vmem()] * (1 + len(flat)),
        out_specs=pl.BlockSpec((PER, rows, BLOCK), lambda i: (i, 0, 0)),
        scratch_shapes=[pltpu.VMEM((cols, BLOCK), F32), pltpu.VMEM((BLOCK, BLOCK), F32)],
        compiler_params=params(),
        cost_estimate=cost(7),
        name="send",
    )(idx, mask, *flat)


def place_pivots(idx_ref, pad, y_ref, g_ref):
    for k in range(NP):
        at = idx_ref[k // PIV * BLOCK + k % PIV]
        if pad:
            at = at + (at >> pad.bit_length() - 1) * PIV
        g_ref[k:k + 1, :] = y_ref[pl.ds(at, 1), :]


def store_pivots(rows, ep_ref, p_ref, q_ref):
    for j in range(NP // BLOCK):
        c = slice(j * BLOCK, (j + 1) * BLOCK)
        blk = jnp.where(ep_ref[BLOCK:BLOCK + 1, c] > 0, rows[c].T, 0.0) + ep_ref[:BLOCK, c]
        p_ref[:, c] = blk
        q_ref[:, c] = blk[:PIV]


def panel_kernel(idx_ref, y_ref, ep_ref, p_ref, q_ref, g_ref):
    place_pivots(idx_ref, 0, y_ref, g_ref)
    store_pivots(g_ref[...], ep_ref, p_ref, q_ref)


def panel_less_kernel(part, idx_ref, y_ref, ep_ref, got_ref, sel_ref, inv_ref, p_ref, q_ref, g_ref, h_ref):
    place_pivots(idx_ref, 0, y_ref, g_ref)
    place_pivots(idx_ref, part, got_ref, h_ref)
    rows = g_ref[...] - dot(h_ref[...], dot(sel_ref[...], inv_ref[...]).T)
    store_pivots(rows, ep_ref, p_ref, q_ref)


def panel(idx, y, ep, part=0, child=()):
    return pl.pallas_call(
        functools.partial(panel_less_kernel, part) if child else panel_kernel,
        out_shape=[jax.ShapeDtypeStruct((BLOCK, NP), F32), jax.ShapeDtypeStruct((PIV, NP), F32)],
        in_specs=[smem()] + [vmem()] * (2 + len(child)),
        out_specs=[vmem(), vmem()],
        scratch_shapes=[pltpu.VMEM((NP, BLOCK), F32)] + [pltpu.VMEM((NP, NP), F32)] * (1 if child else 0),
        compiler_params=params(),
        cost_estimate=cost(3),
        name="panel",
    )(idx, y, ep, *child)


def correct_kernel(part, y_ref, got_ref, sel_ref, inv_ref, yc_ref, m_ref):
    @pl.when(pl.program_id(0) == 0)
    def _():
        m_ref[...] = dot(sel_ref[...], inv_ref[...]).T

    got = got_ref[:, :part, :].reshape(-1, NP)
    yc_ref[...] = y_ref[...] - dot(got, m_ref[...])


def correct(part, y, got, sel, inv):
    rows = y.shape[0] // 4
    return pl.pallas_call(
        functools.partial(correct_kernel, part),
        grid=(4,),
        out_shape=jax.ShapeDtypeStruct(y.shape, F32),
        in_specs=[
            pl.BlockSpec((rows, BLOCK), lambda i: (i, 0)),
            pl.BlockSpec((NF // 4, part + PIV, NP), lambda i: (i, 0, 0)),
            vmem(),
            vmem(),
        ],
        out_specs=pl.BlockSpec((rows, BLOCK), lambda i: (i, 0)),
        scratch_shapes=[pltpu.VMEM((NP, BLOCK), F32)],
        compiler_params=params(),
        cost_estimate=cost(4),
        name="correct",
    )(y, got, sel, inv)


def recv_kernel(level, n, half, idx_ref, mask_ref, y_ref, e_ref, *refs):
    g_ref, buf_ref, sem = refs[-3:]
    step = pl.program_id(0)

    def unit_of(i):
        if level < 2:
            return half * n + i
        z, c = half
        z = idx_ref[F + 1] if z == 0 else 1 - idx_ref[F + 1]
        c = idx_ref[F] if c == 0 else 1 - idx_ref[F]
        return i * 4 + z * 2 + c

    def fetch(i):
        cols = pl.ds(pl.multiple_of(unit_of(i) * UNIT, UNIT), UNIT)
        return pltpu.make_async_copy(e_ref.at[level, 0, :, cols], buf_ref.at[i], sem.at[i])

    @pl.when(step == 0)
    def _():
        for i in range(n):
            fetch(i).start()

    fetch(step).wait()
    unit = unit_of(step)
    for j in range(PER):
        base = (unit * PER + j) * BLOCK
        for k in range(BLOCK):
            g_ref[k:k + 1, :] = y_ref[pl.ds(idx_ref[base + k], 1), :]
        here = mask_ref[pl.ds(unit * PER + j, 1), :]
        c = slice(j * BLOCK, (j + 1) * BLOCK)
        blk = jnp.where(here > 0, g_ref[...].T, 0.0) + buf_ref[step, :, c]
        if level < 2:
            lo, hi = blk[:BLOCK // 2], blk[BLOCK // 2:]
            first = idx_ref[F] == 0
            refs[0][:, c] = jnp.where(first, hi, lo)
            refs[1][:, c] = jnp.where(first, lo, hi)
        else:
            refs[0][:, c] = blk


def recv(level, half, idx, mask, y, entries):
    n, rows, outs = (2, BLOCK, 1) if level == 2 else (4, BLOCK // 2, 2)
    return pl.pallas_call(
        functools.partial(recv_kernel, level, n, half),
        grid=(n,),
        in_specs=[smem(), vmem(), vmem(), pl.BlockSpec(memory_space=pltpu.HBM)],
        out_specs=[pl.BlockSpec((rows, UNIT), lambda i: (0, i))] * outs,
        scratch_shapes=[
            pltpu.VMEM((BLOCK, BLOCK), F32),
            pltpu.VMEM((n, BLOCK, UNIT), F32),
            pltpu.SemaphoreType.DMA((n,)),
        ],
        out_shape=[jax.ShapeDtypeStruct((rows, n * UNIT), F32)] * outs,
        compiler_params=params(),
        cost_estimate=cost(0.9 * n),
        name="recv",
    )(idx, mask, y, entries)


def inv_small(D, n, step):
    rows = lax.broadcasted_iota(jnp.int32, (n, n), 0)
    cols = lax.broadcasted_iota(jnp.int32, (n, n), 1)
    lane = lax.broadcasted_iota(jnp.int32, (1, n), 1)
    for k in range(0, n, step):
        C = [jnp.broadcast_to(D[:, k + j:k + j + 1], (n, n)) for j in range(step)]
        B = [[C[j][k + i:k + i + 1, :] for j in range(step)] for i in range(step)]
        R = []
        for i in range(step):
            unit = jnp.where(lane == k + i, 1.0, 0.0)
            R.append(jnp.where((lane >= k) & (lane < k + step), unit, D[k + i:k + i + 1, :]))
        for p in range(step):
            d = 1.0 / B[p][p]
            for j in range(p + 1, step):
                B[p][j] = B[p][j] * d
            R[p] = R[p] * d
            for i in range(step):
                if i != p:
                    f = B[i][p]
                    for j in range(p + 1, step):
                        B[i][j] = B[i][j] - f * B[p][j]
                    R[i] = R[i] - f * R[p]
        D = jnp.where((cols >= k) & (cols < k + step), 0.0, D)
        for j in range(step):
            D = D - C[j] * R[j]
        for i in range(step):
            D = jnp.where(rows == k + i, R[i], D)
    return D


def inv_kernel(nb, a_ref, o_ref):
    o_ref[...] = a_ref[...].reshape(NP, NP)
    for b in range(NP // nb):
        lo = b * nb
        Ab = o_ref[:, lo:lo + nb]
        Dinv = inv_small(Ab[lo:lo + nb, :], nb, 8)
        lane = lax.broadcasted_iota(jnp.int32, (nb, NP), 1)
        eye = (lane - lo == lax.broadcasted_iota(jnp.int32, (nb, NP), 0)).astype(F32)
        Rb = jnp.where((lane >= lo) & (lane < lo + nb), eye, o_ref[lo:lo + nb, :])
        Rn = dot(Dinv, Rb)
        lane2 = lax.broadcasted_iota(jnp.int32, (NP, NP), 1)
        rest = jnp.where((lane2 >= lo) & (lane2 < lo + nb), 0.0, o_ref[...])
        o_ref[...] = rest - dot(Ab, Rn)
        o_ref[lo:lo + nb, :] = Rn


def inverse(got):
    last = got.shape[1] // PIV - 1
    return pl.pallas_call(
        functools.partial(inv_kernel, 64),
        grid=(1,),
        out_shape=jax.ShapeDtypeStruct((NP, NP), F32),
        in_specs=[pl.BlockSpec((NF, PIV, NP), lambda i: (0, last, 0))],
        out_specs=pl.BlockSpec((NP, NP), lambda i: (0, 0)),
        compiler_params=params(),
        cost_estimate=cost(12),
        name="inverse",
    )(got)


def last_kernel(a_ref, a12_ref, p_ref, inv_ref, m0_ref, m1_ref, mult_ref, top_ref):
    m = dot(p_ref[...], inv_ref[...])
    mult_ref[0] = m0_ref[PIV:, :]
    mult_ref[1] = m1_ref[PIV:, :]
    mult_ref[2] = m[PIV:, :]
    a12 = a12_ref[...].reshape(NP, UNIT)
    s = a_ref[...] - dot(m, a12)
    for j in range(PER):
        top_ref[:, j * UPD:(j + 1) * UPD] = s[PIV:, j * BLOCK + PIV:(j + 1) * BLOCK]


def last(a, a12, p, inv, m0, m1):
    return pl.pallas_call(
        last_kernel,
        out_shape=[jax.ShapeDtypeStruct((3, UPD, NP), F32), jax.ShapeDtypeStruct((UPD, PER * UPD), F32)],
        in_specs=[vmem()] * 6,
        out_specs=[vmem(), vmem()],
        compiler_params=params(),
        cost_estimate=cost(2),
        name="last",
    )(a, a12, p, inv, m0, m1)


def swap(x, axis, d):
    n = lax.axis_size(axis)
    return lax.ppermute(x, axis, [(i, i ^ d) for i in range(n)])


def part_of(x, i, size, dim):
    return lax.dynamic_slice_in_dim(x, i * size, size, dim)


def ordered(bit, mine, other):
    return jnp.where(bit == 0, mine, other), jnp.where(bit == 0, other, mine)


def tie(x, y):
    return lax.optimization_barrier((x, y))


def both_halves(x):
    both = jnp.stack(ordered(lax.axis_index("zh"), x, swap(x, "zh", 1)))
    return jnp.broadcast_to(both[None], (NF // 2,) + both.shape)


def gather_xy(out):
    got = lax.all_to_all(out, ("x", "y"), split_axis=0, concat_axis=0, tiled=True)
    return got.reshape((NF,) + out.shape[2:])


def gather_all(x):
    out = jnp.broadcast_to(x[None], (NF,) + x.shape)
    return lax.all_to_all(out, FRONT, split_axis=0, concat_axis=0, tiled=True)


def shards(child_update, entries, slots):
    zl = lax.axis_index("zl")
    core = lax.axis_index("core")
    z0, z1 = zl & 1, zl >> 1
    front = lax.axis_index("x") * 8 + lax.axis_index("y") * 2 + lax.axis_index("zh")
    leaf = zl * 2 + core
    bits = [(core, "core", 1), (z0, "zl", 1), (z1, "zl", 2)]
    parts = [None, 64, 32]
    splits = [None, core, core * 2 + z0]

    plans = []
    for t in range(3):
        slot = lax.dynamic_index_in_dim(slots[t], (leaf >> t) << t, 0, keepdims=False)
        present = slot >= 0
        at = jnp.maximum(slot, 0)
        plan = {}
        if t == 0:
            col, row, mine = at, at, present
        else:
            blk, pos = at // UPD, at % UPD + PIV
            part, r = parts[t], splits[t]
            col = blk * BLOCK + pos
            mine = present & (pos // part == r)
            row = jnp.where(mine, blk * part + pos - part * r, 0)
            far = jnp.where(mine, blk * (part + PIV) + pos - part * r, 0)
            plan["sel"] = part_of(far, front, BLOCK, 0)
            plan["sel_mask"] = part_of(mine, front, BLOCK, 0).astype(F32)[:, None]
        plan["col"] = col
        plan["col_mask"] = present.astype(F32).reshape(NF, BLOCK)
        plan["row"] = jnp.concatenate([row, jnp.stack([core, z0] + [jnp.zeros_like(core)] * 126)])
        plan["row_mask"] = mine.astype(F32).reshape(NF, BLOCK)
        ep = entries[t, 0].reshape(BLOCK, NF, BLOCK)[:, :, :PIV].reshape(BLOCK, NP)
        piv_mask = plan["row_mask"][:, :PIV].reshape(1, NP)
        plan["ep"] = jnp.concatenate([ep, jnp.broadcast_to(piv_mask, (PIV, NP))])
        plans.append(plan)
    def placed(t, half, y):
        return recv(t, half, plans[t]["row"], plans[t]["row_mask"], y, entries)

    def summed(x, steps):
        for bit, axis, d in steps:
            x = x + swap(x, axis, d)
        return x

    def exchange(out):
        return lax.all_to_all(out, FRONT, split_axis=0, concat_axis=0, tiled=True).reshape(-1, BLOCK)

    y = exchange(send(plans[0]["col"], plans[0]["col_mask"], (child_update[0],)))
    y, plans = tie(y, plans)
    p, _ = panel(plans[0]["row"], y, plans[0]["ep"])
    p = summed(p, bits[:1])
    out = both_halves(jnp.concatenate([part_of(p, core, 64, 0), p[:PIV]], 0))
    y, out = tie(y, out)
    got0 = gather_xy(out)
    src = []
    for h in range(2):
        away, keep = placed(0, h, y)
        src.append((keep, swap(away, "core", 1)))
    out, got0 = tie(send(plans[1]["col"], plans[1]["col_mask"], *src), got0)

    y = exchange(out)
    inv0 = inverse(got0)
    m0 = dot(p, inv0)
    sel = jnp.take(got0.reshape(-1, NP), plans[1]["sel"], axis=0) * plans[1]["sel_mask"]
    child = (got0, summed(sel, bits[:1]), inv0)
    p, _ = panel(plans[1]["row"], y, plans[1]["ep"], 64, (got0.reshape(-1, NP),) + child[1:])
    p = summed(p, bits[:1])
    y = correct(64, y, *child)
    y, p = tie(y, p)
    p = summed(p, bits[1:2])
    away, keep = placed(1, 0, y)
    p, away, keep = lax.optimization_barrier((p, away, keep))
    out = both_halves(jnp.concatenate([part_of(p, splits[2], 32, 0), p[:PIV]], 0))
    src = []
    for h in range(2):
        if h:
            away, keep = placed(1, 1, y)
        rows = keep + swap(away, "core", 1)
        if h:
            rows, out = tie(rows, out)
        piece = part_of(rows, z0, 32, 0), swap(part_of(rows, 1 - z0, 32, 0), "zl", 1)
        if not h:
            piece, out = tie(piece, out)
        src.append(piece)
    got1 = gather_xy(out)
    out, got1 = tie(send(plans[2]["col"], plans[2]["col_mask"], *src), got1)

    y = exchange(out)
    inv1 = inverse(got1)
    m1 = dot(p, inv1)
    sel = jnp.take(got1.reshape(-1, NP), plans[2]["sel"], axis=0) * plans[2]["sel_mask"]
    child = (got1, summed(sel, bits[:2]), inv1)
    p, q = panel(plans[2]["row"], y, plans[2]["ep"], 32, (got1.reshape(-1, NP),) + child[1:])
    q = summed(q, bits)
    y = correct(32, y, *child)
    y, q = tie(y, q)
    gq = gather_all(q)
    far = placed(2, (1, 0), y)[0] + swap(placed(2, (1, 1), y)[0], "core", 1)
    rows = swap(far[:PIV], "zl", 1)
    p = summed(p, bits)
    far, rows, p, gq, y = lax.optimization_barrier((far, rows, p, gq, y))
    near = placed(2, (0, 0), y)[0] + swap(placed(2, (0, 1), y)[0], "core", 1)
    rows = rows + near[:PIV]
    far = swap(far, "zl", 1)
    w = far.shape[1] // 2
    rows = part_of(rows, z1, w, 1) + swap(part_of(rows, 1 - z1, w, 1), "zl", 2)
    out = both_halves(rows)
    A, out = tie(near + far, out)
    a12 = gather_xy(out)
    inv2 = inverse(gq)
    A = part_of(A, z1, w, 1) + swap(part_of(A, 1 - z1, w, 1), "zl", 2)
    mult, top = last(A, a12, p, inv2, m0, m1)
    return mult[None], top


def solution(mesh):
    fine = Mesh(mesh.devices.reshape(4, 2, 4, 4, 2), LEAF + FRONT)
    in_specs = (P(LEAF, FRONT, None), P(None, LEAF, FRONT, None), P())
    out_specs = (P(LEAF, None, FRONT, None), P(FRONT, LEAF))
    return jax.shard_map(shards, mesh=fine, in_specs=in_specs, out_specs=out_specs, check_vma=False)
```

```python
import functools

import jax
import jax.numpy as jnp
from jax import lax
from jax.experimental import pallas as pl
from jax.experimental.pallas import tpu as pltpu
from jax.sharding import Mesh, PartitionSpec as P

F32 = jnp.float32
HIGHEST = lax.Precision.HIGHEST
BLOCK = 128
PIV = 8
UPD = BLOCK - PIV
NF = 32
F = NF * BLOCK
NP = NF * PIV
PER = 4
UNIT = PER * BLOCK
VMEM_LIMIT = 20 << 20
LEAF = ("zl", "core")
FRONT = ("x", "y", "zh")


def vmem():
    return pl.BlockSpec(memory_space=pltpu.VMEM)


def smem():
    return pl.BlockSpec(memory_space=pltpu.SMEM)


def params(limit=VMEM_LIMIT):
    return pltpu.CompilerParams(vmem_limit_bytes=limit)


def cost(us):
    return pl.CostEstimate(flops=0, bytes_accessed=int(us * 3.6e6), transcendentals=0)


def dot(a, b):
    return jnp.dot(a, b, precision=HIGHEST, preferred_element_type=F32)


def send_kernel(rows, pieces, terms, idx_ref, mask_ref, *refs):
    src, (out_ref, t_ref, g_ref) = refs[:-3], refs[-3:]
    step = pl.program_id(0)

    @pl.when(step == 0)
    def _():
        at = 0
        for p in range(pieces):
            for b in range(src[p * terms].shape[1] // BLOCK):
                blk = src[p * terms][:, b * BLOCK:(b + 1) * BLOCK]
                for j in range(1, terms):
                    blk = blk + src[p * terms + j][:, b * BLOCK:(b + 1) * BLOCK]
                if rows < BLOCK:
                    blk = jnp.concatenate([blk, jnp.zeros((BLOCK - rows, BLOCK), F32)], 0)
                t_ref[at:at + BLOCK, :] = blk.T
                at += BLOCK

    for j in range(PER):
        base = (step * PER + j) * BLOCK
        for k in range(BLOCK):
            g_ref[k:k + 1, :] = t_ref[pl.ds(idx_ref[base + k], 1), :]
        here = mask_ref[pl.ds(step * PER + j, 1), :]
        out_ref[j] = jnp.where(here > 0, g_ref[...].T[:rows], 0.0)


def send(idx, mask, *src):
    flat = [x for piece in src for x in piece]
    rows = flat[0].shape[0]
    cols = sum(piece[0].shape[1] for piece in src)
    return pl.pallas_call(
        functools.partial(send_kernel, rows, len(src), len(src[0])),
        grid=(NF // PER,),
        out_shape=jax.ShapeDtypeStruct((NF, rows, BLOCK), F32),
        in_specs=[smem()] + [vmem()] * (1 + len(flat)),
        out_specs=pl.BlockSpec((PER, rows, BLOCK), lambda i: (i, 0, 0)),
        scratch_shapes=[pltpu.VMEM((cols, BLOCK), F32), pltpu.VMEM((BLOCK, BLOCK), F32)],
        compiler_params=params(),
        cost_estimate=cost(7),
        name="send",
    )(idx, mask, *flat)


def place_pivots(idx_ref, pad, y_ref, g_ref):
    for k in range(NP):
        at = idx_ref[k // PIV * BLOCK + k % PIV]
        if pad:
            at = at + (at >> pad.bit_length() - 1) * PIV
        g_ref[k:k + 1, :] = y_ref[pl.ds(at, 1), :]


def store_pivots(rows, ep_ref, p_ref):
    for j in range(NP // BLOCK):
        c = slice(j * BLOCK, (j + 1) * BLOCK)
        p_ref[:, c] = jnp.where(ep_ref[BLOCK:BLOCK + 1, c] > 0, rows[c].T, 0.0) + ep_ref[:BLOCK, c]


def panel_kernel(idx_ref, y_ref, ep_ref, p_ref, g_ref):
    place_pivots(idx_ref, 0, y_ref, g_ref)
    store_pivots(g_ref[...], ep_ref, p_ref)


def panel_less_kernel(part, idx_ref, y_ref, ep_ref, got_ref, sel_ref, inv_ref, p_ref, g_ref, h_ref):
    place_pivots(idx_ref, 0, y_ref, g_ref)
    place_pivots(idx_ref, part, got_ref, h_ref)
    rows = g_ref[...] - dot(h_ref[...], dot(sel_ref[...], inv_ref[...]).T)
    store_pivots(rows, ep_ref, p_ref)


def panel(idx, y, ep, part=0, child=()):
    return pl.pallas_call(
        functools.partial(panel_less_kernel, part) if child else panel_kernel,
        out_shape=jax.ShapeDtypeStruct((BLOCK, NP), F32),
        in_specs=[smem()] + [vmem()] * (2 + len(child)),
        out_specs=vmem(),
        scratch_shapes=[pltpu.VMEM((NP, BLOCK), F32)] + [pltpu.VMEM((NP, NP), F32)] * (1 if child else 0),
        compiler_params=params(),
        cost_estimate=cost(3),
        name="panel",
    )(idx, y, ep, *child)


def correct_kernel(part, y_ref, got_ref, sel_ref, inv_ref, yc_ref, m_ref):
    @pl.when(pl.program_id(0) == 0)
    def _():
        m_ref[...] = dot(sel_ref[...], inv_ref[...]).T

    got = got_ref[:, :part, :].reshape(-1, NP)
    yc_ref[...] = y_ref[...] - dot(got, m_ref[...])


def correct(part, y, got, sel, inv):
    rows = y.shape[0] // 4
    return pl.pallas_call(
        functools.partial(correct_kernel, part),
        grid=(4,),
        out_shape=jax.ShapeDtypeStruct(y.shape, F32),
        in_specs=[
            pl.BlockSpec((rows, BLOCK), lambda i: (i, 0)),
            pl.BlockSpec((NF // 4, part + PIV, NP), lambda i: (i, 0, 0)),
            vmem(),
            vmem(),
        ],
        out_specs=pl.BlockSpec((rows, BLOCK), lambda i: (i, 0)),
        scratch_shapes=[pltpu.VMEM((NP, BLOCK), F32)],
        compiler_params=params(),
        cost_estimate=cost(4),
        name="correct",
    )(y, got, sel, inv)


def recv_kernel(level, n, half, idx_ref, mask_ref, y_ref, e_ref, *refs):
    g_ref, buf_ref, sem = refs[-3:]
    step = pl.program_id(0)

    def unit_of(i):
        if level < 2:
            return half * n + i
        z, c = half
        z = idx_ref[F + 1] if z == 0 else 1 - idx_ref[F + 1]
        c = idx_ref[F] if c == 0 else 1 - idx_ref[F]
        return i * 4 + z * 2 + c

    def fetch(i):
        cols = pl.ds(pl.multiple_of(unit_of(i) * UNIT, UNIT), UNIT)
        return pltpu.make_async_copy(e_ref.at[level, 0, :, cols], buf_ref.at[i], sem.at[i])

    @pl.when(step == 0)
    def _():
        for i in range(n):
            fetch(i).start()

    fetch(step).wait()
    unit = unit_of(step)
    for j in range(PER):
        base = (unit * PER + j) * BLOCK
        for k in range(BLOCK):
            g_ref[k:k + 1, :] = y_ref[pl.ds(idx_ref[base + k], 1), :]
        here = mask_ref[pl.ds(unit * PER + j, 1), :]
        c = slice(j * BLOCK, (j + 1) * BLOCK)
        blk = jnp.where(here > 0, g_ref[...].T, 0.0) + buf_ref[step, :, c]
        if level < 2:
            lo, hi = blk[:BLOCK // 2], blk[BLOCK // 2:]
            first = idx_ref[F] == 0
            refs[0][:, c] = jnp.where(first, hi, lo)
            refs[1][:, c] = jnp.where(first, lo, hi)
        else:
            refs[0][:, c] = blk


def recv(level, half, idx, mask, y, entries):
    n, rows, outs = (2, BLOCK, 1) if level == 2 else (4, BLOCK // 2, 2)
    return pl.pallas_call(
        functools.partial(recv_kernel, level, n, half),
        grid=(n,),
        in_specs=[smem(), vmem(), vmem(), pl.BlockSpec(memory_space=pltpu.HBM)],
        out_specs=[pl.BlockSpec((rows, UNIT), lambda i: (0, i))] * outs,
        scratch_shapes=[
            pltpu.VMEM((BLOCK, BLOCK), F32),
            pltpu.VMEM((n, BLOCK, UNIT), F32),
            pltpu.SemaphoreType.DMA((n,)),
        ],
        out_shape=[jax.ShapeDtypeStruct((rows, n * UNIT), F32)] * outs,
        compiler_params=params(57 << 20),
        cost_estimate=cost(0.9 * n),
        name="recv",
    )(idx, mask, y, entries)


def inv_small(D, n, step):
    rows = lax.broadcasted_iota(jnp.int32, (n, n), 0)
    cols = lax.broadcasted_iota(jnp.int32, (n, n), 1)
    lane = lax.broadcasted_iota(jnp.int32, (1, n), 1)
    for k in range(0, n, step):
        C = [jnp.broadcast_to(D[:, k + j:k + j + 1], (n, n)) for j in range(step)]
        B = [[C[j][k + i:k + i + 1, :] for j in range(step)] for i in range(step)]
        R = []
        for i in range(step):
            unit = jnp.where(lane == k + i, 1.0, 0.0)
            R.append(jnp.where((lane >= k) & (lane < k + step), unit, D[k + i:k + i + 1, :]))
        for p in range(step):
            d = 1.0 / B[p][p]
            for j in range(p + 1, step):
                B[p][j] = B[p][j] * d
            R[p] = R[p] * d
            for i in range(step):
                if i != p:
                    f = B[i][p]
                    for j in range(p + 1, step):
                        B[i][j] = B[i][j] - f * B[p][j]
                    R[i] = R[i] - f * R[p]
        D = jnp.where((cols >= k) & (cols < k + step), 0.0, D)
        for j in range(step):
            D = D - C[j] * R[j]
        for i in range(step):
            D = jnp.where(rows == k + i, R[i], D)
    return D


def inv_kernel(nb, a_ref, o_ref):
    o_ref[...] = a_ref[...].reshape(NP, NP)
    for b in range(NP // nb):
        lo = b * nb
        Ab = o_ref[:, lo:lo + nb]
        Dinv = inv_small(Ab[lo:lo + nb, :], nb, 8)
        lane = lax.broadcasted_iota(jnp.int32, (nb, NP), 1)
        eye = (lane - lo == lax.broadcasted_iota(jnp.int32, (nb, NP), 0)).astype(F32)
        Rb = jnp.where((lane >= lo) & (lane < lo + nb), eye, o_ref[lo:lo + nb, :])
        Rn = dot(Dinv, Rb)
        lane2 = lax.broadcasted_iota(jnp.int32, (NP, NP), 1)
        rest = jnp.where((lane2 >= lo) & (lane2 < lo + nb), 0.0, o_ref[...])
        o_ref[...] = rest - dot(Ab, Rn)
        o_ref[lo:lo + nb, :] = Rn


def inverse(got, first=0):
    last = got.shape[1] // PIV - 1
    return pl.pallas_call(
        functools.partial(inv_kernel, 64),
        grid=(1,),
        out_shape=jax.ShapeDtypeStruct((NP, NP), F32),
        in_specs=[pl.BlockSpec((NF, PIV, NP), lambda i: (0, last, first // NP))],
        out_specs=pl.BlockSpec((NP, NP), lambda i: (0, 0)),
        compiler_params=params(),
        cost_estimate=cost(12),
        name="inverse",
    )(got)


def last_kernel(a_ref, a12_ref, p_ref, inv_ref, m0_ref, m1_ref, mult_ref, top_ref):
    m = dot(p_ref[...], inv_ref[...])
    mult_ref[0] = m0_ref[PIV:, :]
    mult_ref[1] = m1_ref[PIV:, :]
    mult_ref[2] = m[PIV:, :]
    a12 = a12_ref[:, :, :UNIT].reshape(NP, UNIT)
    s = a_ref[...] - dot(m, a12)
    for j in range(PER):
        top_ref[:, j * UPD:(j + 1) * UPD] = s[PIV:, j * BLOCK + PIV:(j + 1) * BLOCK]


def last(a, a12, p, inv, m0, m1):
    return pl.pallas_call(
        last_kernel,
        out_shape=[jax.ShapeDtypeStruct((3, UPD, NP), F32), jax.ShapeDtypeStruct((UPD, PER * UPD), F32)],
        in_specs=[vmem()] * 6,
        out_specs=[vmem(), vmem()],
        compiler_params=params(),
        cost_estimate=cost(2),
        name="last",
    )(a, a12, p, inv, m0, m1)


def swap(x, axis, d):
    n = lax.axis_size(axis)
    return lax.ppermute(x, axis, [(i, i ^ d) for i in range(n)])


def part_of(x, i, size, dim):
    return lax.dynamic_slice_in_dim(x, i * size, size, dim)


def ordered(bit, mine, other):
    return jnp.where(bit == 0, mine, other), jnp.where(bit == 0, other, mine)


def tie(x, y):
    return lax.optimization_barrier((x, y))


def both_halves(x):
    both = jnp.stack(ordered(lax.axis_index("zh"), x, swap(x, "zh", 1)))
    return jnp.broadcast_to(both[None], (NF // 2,) + both.shape)


def gather_xy(out):
    got = lax.all_to_all(out, ("x", "y"), split_axis=0, concat_axis=0, tiled=True)
    return got.reshape((NF,) + out.shape[2:])


def shards(child_update, entries, slots):
    zl = lax.axis_index("zl")
    core = lax.axis_index("core")
    z0, z1 = zl & 1, zl >> 1
    front = lax.axis_index("x") * 8 + lax.axis_index("y") * 2 + lax.axis_index("zh")
    leaf = zl * 2 + core
    bits = [(core, "core", 1), (z0, "zl", 1), (z1, "zl", 2)]
    parts = [None, 64, 32]
    splits = [None, core, core * 2 + z0]

    plans = []
    for t in range(3):
        slot = lax.dynamic_index_in_dim(slots[t], (leaf >> t) << t, 0, keepdims=False)
        present = slot >= 0
        at = jnp.maximum(slot, 0)
        plan = {}
        if t == 0:
            col, row, mine = at, at, present
        else:
            blk, pos = at // UPD, at % UPD + PIV
            part, r = parts[t], splits[t]
            col = blk * BLOCK + pos
            mine = present & (pos // part == r)
            row = jnp.where(mine, blk * part + pos - part * r, 0)
            far = jnp.where(mine, blk * (part + PIV) + pos - part * r, 0)
            plan["sel"] = part_of(far, front, BLOCK, 0)
            plan["sel_mask"] = part_of(mine, front, BLOCK, 0).astype(F32)[:, None]
        plan["col"] = col
        plan["col_mask"] = present.astype(F32).reshape(NF, BLOCK)
        plan["row"] = jnp.concatenate([row, jnp.stack([core, z0] + [jnp.zeros_like(core)] * 126)])
        plan["row_mask"] = mine.astype(F32).reshape(NF, BLOCK)
        ep = entries[t, 0].reshape(BLOCK, NF, BLOCK)[:, :, :PIV].reshape(BLOCK, NP)
        piv_mask = plan["row_mask"][:, :PIV].reshape(1, NP)
        plan["ep"] = jnp.concatenate([ep, jnp.broadcast_to(piv_mask, (PIV, NP))])
        plans.append(plan)
    def placed(t, half, y):
        return recv(t, half, plans[t]["row"], plans[t]["row_mask"], y, entries)

    def summed(x, steps):
        for bit, axis, d in steps:
            x = x + swap(x, axis, d)
        return x

    def exchange(out):
        return lax.all_to_all(out, FRONT, split_axis=0, concat_axis=0, tiled=True).reshape(-1, BLOCK)

    y = exchange(send(plans[0]["col"], plans[0]["col_mask"], (child_update[0],)))
    y, plans = tie(y, plans)
    p = panel(plans[0]["row"], y, plans[0]["ep"])
    p = summed(p, bits[:1])
    out = both_halves(jnp.concatenate([part_of(p, core, 64, 0), p[:PIV]], 0))
    y, out = tie(y, out)
    got0 = gather_xy(out)
    src = []
    for h in range(2):
        away, keep = placed(0, h, y)
        src.append((keep, swap(away, "core", 1)))
    out, got0 = tie(send(plans[1]["col"], plans[1]["col_mask"], *src), got0)

    y = exchange(out)
    inv0 = inverse(got0)
    m0 = dot(p, inv0)
    sel = jnp.take(got0.reshape(-1, NP), plans[1]["sel"], axis=0) * plans[1]["sel_mask"]
    child = (got0, summed(sel, bits[:1]), inv0)
    p = panel(plans[1]["row"], y, plans[1]["ep"], 64, (got0.reshape(-1, NP),) + child[1:])
    p = summed(p, bits[:1])
    y = correct(64, y, *child)
    y, p = tie(y, p)
    p = summed(p, bits[1:2])
    away, keep = placed(1, 0, y)
    p, away, keep = lax.optimization_barrier((p, away, keep))
    out = both_halves(jnp.concatenate([part_of(p, splits[2], 32, 0), p[:PIV]], 0))
    out, second = tie(out, placed(1, 1, y))
    src = []
    for away, keep in ((away, keep), second):
        rows = keep + swap(away, "core", 1)
        if not src:
            rows, out = tie(rows, out)
        src.append((part_of(rows, z0, 32, 0), swap(part_of(rows, 1 - z0, 32, 0), "zl", 1)))
    got1 = gather_xy(out)
    out, got1 = tie(send(plans[2]["col"], plans[2]["col_mask"], *src), got1)

    y = exchange(out)
    inv1 = inverse(got1)
    m1 = dot(p, inv1)
    sel = jnp.take(got1.reshape(-1, NP), plans[2]["sel"], axis=0) * plans[2]["sel_mask"]
    child = (got1, summed(sel, bits[:2]), inv1)
    p = panel(plans[2]["row"], y, plans[2]["ep"], 32, (got1.reshape(-1, NP),) + child[1:])
    y = correct(32, y, *child)
    away = placed(2, (1, 1), y)[0]
    p, away = tie(summed(p, bits[:1]), away)
    far = placed(2, (1, 0), y)[0]
    p, far = tie(summed(p, bits[1:2]), far)
    far = far + swap(away, "core", 1)
    rows = swap(far[:PIV], "zl", 1)
    away = placed(2, (0, 1), y)[0]
    p, away = tie(summed(p, bits[2:]), away)
    rows, far, away = lax.optimization_barrier((rows, far, away))
    far = swap(far, "zl", 1)
    near = placed(2, (0, 0), y)[0] + swap(away, "core", 1)
    rows = rows + near[:PIV]
    w = far.shape[1] // 2
    rows = part_of(rows, z1, w, 1) + swap(part_of(rows, 1 - z1, w, 1), "zl", 2)
    got = gather_xy(both_halves(jnp.concatenate([rows, p[:PIV]], 1)))
    A = near + far
    A = part_of(A, z1, w, 1) + swap(part_of(A, 1 - z1, w, 1), "zl", 2)
    mult, top = last(A, got, p, inverse(got, w), m0, m1)
    return mult[None], top


def solution(mesh):
    fine = Mesh(mesh.devices.reshape(4, 2, 4, 4, 2), LEAF + FRONT)
    in_specs = (P(LEAF, FRONT, None), P(None, LEAF, FRONT, None), P())
    out_specs = (P(LEAF, None, FRONT, None), P(FRONT, LEAF))
    return jax.shard_map(shards, mesh=fine, in_specs=in_specs, out_specs=out_specs, check_vma=False)
```

```python
import functools

import jax
import jax.numpy as jnp
from jax import lax
from jax.experimental import pallas as pl
from jax.experimental.pallas import tpu as pltpu
from jax.sharding import Mesh, PartitionSpec as P

F32 = jnp.float32
HIGHEST = lax.Precision.HIGHEST
BLOCK = 128
PIV = 8
UPD = BLOCK - PIV
NF = 32
F = NF * BLOCK
NP = NF * PIV
PER = 4
UNIT = PER * BLOCK
VMEM_LIMIT = 20 << 20
LEAF = ("zl", "core")
FRONT = ("x", "y", "zh")


def vmem():
    return pl.BlockSpec(memory_space=pltpu.VMEM)


def smem():
    return pl.BlockSpec(memory_space=pltpu.SMEM)


def params():
    return pltpu.CompilerParams(vmem_limit_bytes=VMEM_LIMIT)


def cost(us):
    return pl.CostEstimate(flops=0, bytes_accessed=int(us * 3.6e6), transcendentals=0)


def dot(a, b):
    return jnp.dot(a, b, precision=HIGHEST, preferred_element_type=F32)


def send_kernel(rows, pieces, terms, idx_ref, mask_ref, *refs):
    src, (out_ref, t_ref, g_ref) = refs[:-3], refs[-3:]
    step = pl.program_id(0)

    @pl.when(step == 0)
    def _():
        at = 0
        for p in range(pieces):
            for b in range(src[p * terms].shape[1] // BLOCK):
                blk = src[p * terms][:, b * BLOCK:(b + 1) * BLOCK]
                for j in range(1, terms):
                    blk = blk + src[p * terms + j][:, b * BLOCK:(b + 1) * BLOCK]
                if rows < BLOCK:
                    blk = jnp.concatenate([blk, jnp.zeros((BLOCK - rows, BLOCK), F32)], 0)
                t_ref[at:at + BLOCK, :] = blk.T
                at += BLOCK

    for j in range(PER):
        base = (step * PER + j) * BLOCK
        for k in range(BLOCK):
            g_ref[k:k + 1, :] = t_ref[pl.ds(idx_ref[base + k], 1), :]
        here = mask_ref[pl.ds(step * PER + j, 1), :]
        out_ref[j] = jnp.where(here > 0, g_ref[...].T[:rows], 0.0)


def send(idx, mask, *src):
    flat = [x for piece in src for x in piece]
    rows = flat[0].shape[0]
    cols = sum(piece[0].shape[1] for piece in src)
    return pl.pallas_call(
        functools.partial(send_kernel, rows, len(src), len(src[0])),
        grid=(NF // PER,),
        out_shape=jax.ShapeDtypeStruct((NF, rows, BLOCK), F32),
        in_specs=[smem()] + [vmem()] * (1 + len(flat)),
        out_specs=pl.BlockSpec((PER, rows, BLOCK), lambda i: (i, 0, 0)),
        scratch_shapes=[pltpu.VMEM((cols, BLOCK), F32), pltpu.VMEM((BLOCK, BLOCK), F32)],
        compiler_params=params(),
        cost_estimate=cost(7),
        name="send",
    )(idx, mask, *flat)


def place_pivots(idx_ref, pad, y_ref, g_ref):
    for k in range(NP):
        at = idx_ref[k // PIV * BLOCK + k % PIV]
        if pad:
            at = at + (at >> pad.bit_length() - 1) * PIV
        g_ref[k:k + 1, :] = y_ref[pl.ds(at, 1), :]


def store_pivots(rows, ep_ref, p_ref):
    for j in range(NP // BLOCK):
        c = slice(j * BLOCK, (j + 1) * BLOCK)
        p_ref[:, c] = jnp.where(ep_ref[BLOCK:BLOCK + 1, c] > 0, rows[c].T, 0.0) + ep_ref[:BLOCK, c]


def panel_kernel(idx_ref, y_ref, ep_ref, p_ref, g_ref):
    place_pivots(idx_ref, 0, y_ref, g_ref)
    store_pivots(g_ref[...], ep_ref, p_ref)


def panel_less_kernel(part, idx_ref, y_ref, ep_ref, got_ref, sel_ref, inv_ref, p_ref, g_ref, h_ref):
    place_pivots(idx_ref, 0, y_ref, g_ref)
    place_pivots(idx_ref, part, got_ref, h_ref)
    rows = g_ref[...] - dot(h_ref[...], dot(sel_ref[...], inv_ref[...]).T)
    store_pivots(rows, ep_ref, p_ref)


def panel(idx, y, ep, part=0, child=()):
    return pl.pallas_call(
        functools.partial(panel_less_kernel, part) if child else panel_kernel,
        out_shape=jax.ShapeDtypeStruct((BLOCK, NP), F32),
        in_specs=[smem()] + [vmem()] * (2 + len(child)),
        out_specs=vmem(),
        scratch_shapes=[pltpu.VMEM((NP, BLOCK), F32)] + [pltpu.VMEM((NP, NP), F32)] * (1 if child else 0),
        compiler_params=params(),
        cost_estimate=cost(3),
        name="panel",
    )(idx, y, ep, *child)


def correct_kernel(part, y_ref, got_ref, sel_ref, inv_ref, yc_ref, m_ref):
    @pl.when(pl.program_id(0) == 0)
    def _():
        m_ref[...] = dot(sel_ref[...], inv_ref[...]).T

    got = got_ref[:, :part, :].reshape(-1, NP)
    yc_ref[...] = y_ref[...] - dot(got, m_ref[...])


def correct(part, y, got, sel, inv):
    rows = y.shape[0] // 4
    return pl.pallas_call(
        functools.partial(correct_kernel, part),
        grid=(4,),
        out_shape=jax.ShapeDtypeStruct(y.shape, F32),
        in_specs=[
            pl.BlockSpec((rows, BLOCK), lambda i: (i, 0)),
            pl.BlockSpec((NF // 4, part + PIV, NP), lambda i: (i, 0, 0)),
            vmem(),
            vmem(),
        ],
        out_specs=pl.BlockSpec((rows, BLOCK), lambda i: (i, 0)),
        scratch_shapes=[pltpu.VMEM((NP, BLOCK), F32)],
        compiler_params=params(),
        cost_estimate=cost(4),
        name="correct",
    )(y, got, sel, inv)


def recv_kernel(level, n, half, idx_ref, mask_ref, y_ref, e_ref, *refs):
    g_ref = refs[-1]
    i = pl.program_id(0)
    if level < 2:
        unit = half * n + i
    else:
        z, c = half
        z = idx_ref[F + 1] if z == 0 else 1 - idx_ref[F + 1]
        c = idx_ref[F] if c == 0 else 1 - idx_ref[F]
        unit = i * 4 + z * 2 + c
    for j in range(PER):
        base = (unit * PER + j) * BLOCK
        for k in range(BLOCK):
            g_ref[k:k + 1, :] = y_ref[pl.ds(idx_ref[base + k], 1), :]
        here = mask_ref[pl.ds(unit * PER + j, 1), :]
        c = slice(j * BLOCK, (j + 1) * BLOCK)
        at = pl.ds(pl.multiple_of(base, BLOCK), BLOCK)
        blk = jnp.where(here > 0, g_ref[...].T, 0.0) + e_ref[:, at]
        if level < 2:
            lo, hi = blk[:BLOCK // 2], blk[BLOCK // 2:]
            first = idx_ref[F] == 0
            refs[0][:, c] = jnp.where(first, hi, lo)
            refs[1][:, c] = jnp.where(first, lo, hi)
        else:
            refs[0][:, c] = blk


def recv(level, half, idx, mask, y, entries):
    n, rows, outs = (2, BLOCK, 1) if level == 2 else (4, BLOCK // 2, 2)
    return pl.pallas_call(
        functools.partial(recv_kernel, level, n, half),
        grid=(n,),
        in_specs=[smem(), vmem(), vmem(), vmem()],
        out_specs=[pl.BlockSpec((rows, UNIT), lambda i: (0, i))] * outs,
        scratch_shapes=[pltpu.VMEM((BLOCK, BLOCK), F32)],
        out_shape=[jax.ShapeDtypeStruct((rows, n * UNIT), F32)] * outs,
        compiler_params=params(),
        cost_estimate=cost(0.9 * n),
        name="recv",
    )(idx, mask, y, entries)


def inv_small(D, n, step):
    rows = lax.broadcasted_iota(jnp.int32, (n, n), 0)
    cols = lax.broadcasted_iota(jnp.int32, (n, n), 1)
    lane = lax.broadcasted_iota(jnp.int32, (1, n), 1)
    for k in range(0, n, step):
        C = [jnp.broadcast_to(D[:, k + j:k + j + 1], (n, n)) for j in range(step)]
        B = [[C[j][k + i:k + i + 1, :] for j in range(step)] for i in range(step)]
        R = []
        for i in range(step):
            unit = jnp.where(lane == k + i, 1.0, 0.0)
            R.append(jnp.where((lane >= k) & (lane < k + step), unit, D[k + i:k + i + 1, :]))
        for p in range(step):
            d = 1.0 / B[p][p]
            for j in range(p + 1, step):
                B[p][j] = B[p][j] * d
            R[p] = R[p] * d
            for i in range(step):
                if i != p:
                    f = B[i][p]
                    for j in range(p + 1, step):
                        B[i][j] = B[i][j] - f * B[p][j]
                    R[i] = R[i] - f * R[p]
        D = jnp.where((cols >= k) & (cols < k + step), 0.0, D)
        for j in range(step):
            D = D - C[j] * R[j]
        for i in range(step):
            D = jnp.where(rows == k + i, R[i], D)
    return D


def inv_kernel(nb, a_ref, o_ref):
    o_ref[...] = a_ref[...].reshape(NP, NP)
    for b in range(NP // nb):
        lo = b * nb
        Ab = o_ref[:, lo:lo + nb]
        Dinv = inv_small(Ab[lo:lo + nb, :], nb, 8)
        lane = lax.broadcasted_iota(jnp.int32, (nb, NP), 1)
        eye = (lane - lo == lax.broadcasted_iota(jnp.int32, (nb, NP), 0)).astype(F32)
        Rb = jnp.where((lane >= lo) & (lane < lo + nb), eye, o_ref[lo:lo + nb, :])
        Rn = dot(Dinv, Rb)
        lane2 = lax.broadcasted_iota(jnp.int32, (NP, NP), 1)
        rest = jnp.where((lane2 >= lo) & (lane2 < lo + nb), 0.0, o_ref[...])
        o_ref[...] = rest - dot(Ab, Rn)
        o_ref[lo:lo + nb, :] = Rn


def inverse(got, first=0):
    last = got.shape[1] // PIV - 1
    return pl.pallas_call(
        functools.partial(inv_kernel, 64),
        grid=(1,),
        out_shape=jax.ShapeDtypeStruct((NP, NP), F32),
        in_specs=[pl.BlockSpec((NF, PIV, NP), lambda i: (0, last, first // NP))],
        out_specs=pl.BlockSpec((NP, NP), lambda i: (0, 0)),
        compiler_params=params(),
        cost_estimate=cost(12),
        name="inverse",
    )(got)


def last_kernel(a_ref, a12_ref, p_ref, inv_ref, m0_ref, m1_ref, mult_ref, top_ref):
    m = dot(p_ref[...], inv_ref[...])
    mult_ref[0] = m0_ref[PIV:, :]
    mult_ref[1] = m1_ref[PIV:, :]
    mult_ref[2] = m[PIV:, :]
    a12 = a12_ref[:, :, :UNIT].reshape(NP, UNIT)
    s = a_ref[...] - dot(m, a12)
    for j in range(PER):
        top_ref[:, j * UPD:(j + 1) * UPD] = s[PIV:, j * BLOCK + PIV:(j + 1) * BLOCK]


def last(a, a12, p, inv, m0, m1):
    return pl.pallas_call(
        last_kernel,
        out_shape=[jax.ShapeDtypeStruct((3, UPD, NP), F32), jax.ShapeDtypeStruct((UPD, PER * UPD), F32)],
        in_specs=[vmem()] * 6,
        out_specs=[vmem(), vmem()],
        compiler_params=params(),
        cost_estimate=cost(2),
        name="last",
    )(a, a12, p, inv, m0, m1)


def swap(x, axis, d):
    n = lax.axis_size(axis)
    return lax.ppermute(x, axis, [(i, i ^ d) for i in range(n)])


def part_of(x, i, size, dim):
    return lax.dynamic_slice_in_dim(x, i * size, size, dim)


def ordered(bit, mine, other):
    return jnp.where(bit == 0, mine, other), jnp.where(bit == 0, other, mine)


def tie(x, y):
    return lax.optimization_barrier((x, y))


def both_halves(x):
    both = jnp.stack(ordered(lax.axis_index("zh"), x, swap(x, "zh", 1)))
    return jnp.broadcast_to(both[None], (NF // 2,) + both.shape)


def gather_xy(out):
    got = lax.all_to_all(out, ("x", "y"), split_axis=0, concat_axis=0, tiled=True)
    return got.reshape((NF,) + out.shape[2:])


def shards(child_update, entries, slots):
    zl = lax.axis_index("zl")
    core = lax.axis_index("core")
    z0, z1 = zl & 1, zl >> 1
    front = lax.axis_index("x") * 8 + lax.axis_index("y") * 2 + lax.axis_index("zh")
    leaf = zl * 2 + core
    bits = [(core, "core", 1), (z0, "zl", 1), (z1, "zl", 2)]
    parts = [None, 64, 32]
    splits = [None, core, core * 2 + z0]

    plans = []
    for t in range(3):
        slot = lax.dynamic_index_in_dim(slots[t], (leaf >> t) << t, 0, keepdims=False)
        present = slot >= 0
        at = jnp.maximum(slot, 0)
        plan = {}
        if t == 0:
            col, row, mine = at, at, present
        else:
            blk, pos = at // UPD, at % UPD + PIV
            part, r = parts[t], splits[t]
            col = blk * BLOCK + pos
            mine = present & (pos // part == r)
            row = jnp.where(mine, blk * part + pos - part * r, 0)
            far = jnp.where(mine, blk * (part + PIV) + pos - part * r, 0)
            plan["sel"] = part_of(far, front, BLOCK, 0)
            plan["sel_mask"] = part_of(mine, front, BLOCK, 0).astype(F32)[:, None]
        plan["col"] = col
        plan["col_mask"] = present.astype(F32).reshape(NF, BLOCK)
        plan["row"] = jnp.concatenate([row, jnp.stack([core, z0] + [jnp.zeros_like(core)] * 126)])
        plan["row_mask"] = mine.astype(F32).reshape(NF, BLOCK)
        ep = entries[t, 0].reshape(BLOCK, NF, BLOCK)[:, :, :PIV].reshape(BLOCK, NP)
        plan["entries"] = entries[t, 0]
        piv_mask = plan["row_mask"][:, :PIV].reshape(1, NP)
        plan["ep"] = jnp.concatenate([ep, jnp.broadcast_to(piv_mask, (PIV, NP))])
        plans.append(plan)
    def placed(t, half, y):
        return recv(t, half, plans[t]["row"], plans[t]["row_mask"], y, plans[t]["entries"])

    def summed(x, steps):
        for bit, axis, d in steps:
            x = x + swap(x, axis, d)
        return x

    def exchange(out):
        return lax.all_to_all(out, FRONT, split_axis=0, concat_axis=0, tiled=True).reshape(-1, BLOCK)

    y = exchange(send(plans[0]["col"], plans[0]["col_mask"], (child_update[0],)))
    y, plans = tie(y, plans)
    p = panel(plans[0]["row"], y, plans[0]["ep"])
    p = summed(p, bits[:1])
    out = both_halves(jnp.concatenate([part_of(p, core, 64, 0), p[:PIV]], 0))
    y, out = tie(y, out)
    got0 = gather_xy(out)
    src = []
    for h in range(2):
        away, keep = placed(0, h, y)
        src.append((keep, swap(away, "core", 1)))
    out, got0 = tie(send(plans[1]["col"], plans[1]["col_mask"], *src), got0)

    y = exchange(out)
    inv0 = inverse(got0)
    m0 = dot(p, inv0)
    sel = jnp.take(got0.reshape(-1, NP), plans[1]["sel"], axis=0) * plans[1]["sel_mask"]
    child = (got0, summed(sel, bits[:1]), inv0)
    p = panel(plans[1]["row"], y, plans[1]["ep"], 64, (got0.reshape(-1, NP),) + child[1:])
    p = summed(p, bits[:1])
    y = correct(64, y, *child)
    y, p = tie(y, p)
    p = summed(p, bits[1:2])
    away, keep = placed(1, 0, y)
    p, away, keep = lax.optimization_barrier((p, away, keep))
    out = both_halves(jnp.concatenate([part_of(p, splits[2], 32, 0), p[:PIV]], 0))
    out, second = tie(out, placed(1, 1, y))
    got1 = gather_xy(out)
    src = []
    for away, keep in ((away, keep), second):
        rows = keep + swap(away, "core", 1)
        src.append((part_of(rows, z0, 32, 0), swap(part_of(rows, 1 - z0, 32, 0), "zl", 1)))
    out, got1 = tie(send(plans[2]["col"], plans[2]["col_mask"], *src), got1)

    y = exchange(out)
    inv1 = inverse(got1)
    m1 = dot(p, inv1)
    sel = jnp.take(got1.reshape(-1, NP), plans[2]["sel"], axis=0) * plans[2]["sel_mask"]
    child = (got1, summed(sel, bits[:2]), inv1)
    p = panel(plans[2]["row"], y, plans[2]["ep"], 32, (got1.reshape(-1, NP),) + child[1:])
    y = correct(32, y, *child)
    away = placed(2, (1, 1), y)[0]
    p, away = tie(summed(p, bits[:1]), away)
    far = placed(2, (1, 0), y)[0]
    p, far = tie(summed(p, bits[1:2]), far)
    far = far + swap(away, "core", 1)
    rows = swap(far[:PIV], "zl", 1)
    away = placed(2, (0, 1), y)[0]
    p, away = tie(summed(p, bits[2:]), away)
    rows, far, away = lax.optimization_barrier((rows, far, away))
    far = swap(far, "zl", 1)
    near = placed(2, (0, 0), y)[0] + swap(away, "core", 1)
    rows = rows + near[:PIV]
    w = far.shape[1] // 2
    rows = part_of(rows, z1, w, 1) + swap(part_of(rows, 1 - z1, w, 1), "zl", 2)
    out = both_halves(jnp.concatenate([rows, p[:PIV]], 1))
    far, out = tie(far, out)
    got = gather_xy(out)
    A = near + far
    A = part_of(A, z1, w, 1) + swap(part_of(A, 1 - z1, w, 1), "zl", 2)
    A, got = tie(A, got)
    mult, top = last(A, got, p, inverse(got, w), m0, m1)
    return mult[None], top


def solution(mesh):
    fine = Mesh(mesh.devices.reshape(4, 2, 4, 4, 2), LEAF + FRONT)
    in_specs = (P(LEAF, FRONT, None), P(None, LEAF, FRONT, None), P())
    out_specs = (P(LEAF, None, FRONT, None), P(FRONT, LEAF))
    return jax.shard_map(shards, mesh=fine, in_specs=in_specs, out_specs=out_specs, check_vma=False)
```

```python
import functools

import jax
import jax.numpy as jnp
from jax import lax
from jax.experimental import pallas as pl
from jax.experimental.pallas import tpu as pltpu
from jax.sharding import Mesh, PartitionSpec as P

F32 = jnp.float32
HIGHEST = lax.Precision.HIGHEST
BLOCK = 128
PIV = 8
UPD = BLOCK - PIV
NF = 32
F = NF * BLOCK
NP = NF * PIV
PER = 4
UNIT = PER * BLOCK
VMEM_LIMIT = 20 << 20
LEAF = ("zl", "core")
FRONT = ("x", "y", "zh")


def vmem():
    return pl.BlockSpec(memory_space=pltpu.VMEM)


def smem():
    return pl.BlockSpec(memory_space=pltpu.SMEM)


def params():
    return pltpu.CompilerParams(vmem_limit_bytes=VMEM_LIMIT)


def cost(us):
    return pl.CostEstimate(flops=0, bytes_accessed=int(us * 3.6e6), transcendentals=0)


def dot(a, b):
    return jnp.dot(a, b, precision=HIGHEST, preferred_element_type=F32)


def send_kernel(rows, pieces, terms, idx_ref, mask_ref, *refs):
    src, (out_ref, t_ref, g_ref) = refs[:-3], refs[-3:]
    step = pl.program_id(0)

    @pl.when(step == 0)
    def _():
        at = 0
        for p in range(pieces):
            for b in range(src[p * terms].shape[1] // BLOCK):
                blk = src[p * terms][:, b * BLOCK:(b + 1) * BLOCK]
                for j in range(1, terms):
                    blk = blk + src[p * terms + j][:, b * BLOCK:(b + 1) * BLOCK]
                if rows < BLOCK:
                    blk = jnp.concatenate([blk, jnp.zeros((BLOCK - rows, BLOCK), F32)], 0)
                t_ref[at:at + BLOCK, :] = blk.T
                at += BLOCK

    for j in range(PER):
        base = (step * PER + j) * BLOCK
        for k in range(BLOCK):
            g_ref[k:k + 1, :] = t_ref[pl.ds(idx_ref[base + k], 1), :]
        here = mask_ref[pl.ds(step * PER + j, 1), :]
        out_ref[j] = jnp.where(here > 0, g_ref[...].T[:rows], 0.0)


def send(idx, mask, *src):
    flat = [x for piece in src for x in piece]
    rows = flat[0].shape[0]
    cols = sum(piece[0].shape[1] for piece in src)
    return pl.pallas_call(
        functools.partial(send_kernel, rows, len(src), len(src[0])),
        grid=(NF // PER,),
        out_shape=jax.ShapeDtypeStruct((NF, rows, BLOCK), F32),
        in_specs=[smem()] + [vmem()] * (1 + len(flat)),
        out_specs=pl.BlockSpec((PER, rows, BLOCK), lambda i: (i, 0, 0)),
        scratch_shapes=[pltpu.VMEM((cols, BLOCK), F32), pltpu.VMEM((BLOCK, BLOCK), F32)],
        compiler_params=params(),
        cost_estimate=cost(7),
        name="send",
    )(idx, mask, *flat)


def place_pivots(idx_ref, pad, y_ref, g_ref):
    for k in range(NP):
        at = idx_ref[k // PIV * BLOCK + k % PIV]
        if pad:
            at = at + (at >> pad.bit_length() - 1) * PIV
        g_ref[k:k + 1, :] = y_ref[pl.ds(at, 1), :]


def store_pivots(rows, ep_ref, p_ref):
    for j in range(NP // BLOCK):
        c = slice(j * BLOCK, (j + 1) * BLOCK)
        p_ref[:, c] = jnp.where(ep_ref[BLOCK:BLOCK + 1, c] > 0, rows[c].T, 0.0) + ep_ref[:BLOCK, c]


def panel_kernel(idx_ref, y_ref, ep_ref, p_ref, g_ref):
    place_pivots(idx_ref, 0, y_ref, g_ref)
    store_pivots(g_ref[...], ep_ref, p_ref)


def panel_less_kernel(part, idx_ref, y_ref, ep_ref, got_ref, sel_ref, inv_ref, p_ref, g_ref, h_ref):
    place_pivots(idx_ref, 0, y_ref, g_ref)
    place_pivots(idx_ref, part, got_ref, h_ref)
    rows = g_ref[...] - dot(h_ref[...], dot(sel_ref[...], inv_ref[...]).T)
    store_pivots(rows, ep_ref, p_ref)


def panel(idx, y, ep, part=0, child=()):
    return pl.pallas_call(
        functools.partial(panel_less_kernel, part) if child else panel_kernel,
        out_shape=jax.ShapeDtypeStruct((BLOCK, NP), F32),
        in_specs=[smem()] + [vmem()] * (2 + len(child)),
        out_specs=vmem(),
        scratch_shapes=[pltpu.VMEM((NP, BLOCK), F32)] + [pltpu.VMEM((NP, NP), F32)] * (1 if child else 0),
        compiler_params=params(),
        cost_estimate=cost(3),
        name="panel",
    )(idx, y, ep, *child)


def correct_kernel(part, y_ref, got_ref, sel_ref, inv_ref, yc_ref, m_ref):
    @pl.when(pl.program_id(0) == 0)
    def _():
        m_ref[...] = dot(sel_ref[...], inv_ref[...]).T

    got = got_ref[:, :part, :].reshape(-1, NP)
    yc_ref[...] = y_ref[...] - dot(got, m_ref[...])


def correct(part, y, got, sel, inv):
    rows = y.shape[0] // 4
    return pl.pallas_call(
        functools.partial(correct_kernel, part),
        grid=(4,),
        out_shape=jax.ShapeDtypeStruct(y.shape, F32),
        in_specs=[
            pl.BlockSpec((rows, BLOCK), lambda i: (i, 0)),
            pl.BlockSpec((NF // 4, part + PIV, NP), lambda i: (i, 0, 0)),
            vmem(),
            vmem(),
        ],
        out_specs=pl.BlockSpec((rows, BLOCK), lambda i: (i, 0)),
        scratch_shapes=[pltpu.VMEM((NP, BLOCK), F32)],
        compiler_params=params(),
        cost_estimate=cost(4),
        name="correct",
    )(y, got, sel, inv)


def recv_kernel(level, n, half, idx_ref, mask_ref, y_ref, e_ref, *refs):
    g_ref = refs[-1]
    i = pl.program_id(0)
    if level < 2:
        unit = half * n + i
    else:
        z, c = half
        z = idx_ref[F + 1] if z == 0 else 1 - idx_ref[F + 1]
        c = idx_ref[F] if c == 0 else 1 - idx_ref[F]
        unit = i * 4 + z * 2 + c
    for j in range(PER):
        base = (unit * PER + j) * BLOCK
        for k in range(BLOCK):
            g_ref[k:k + 1, :] = y_ref[pl.ds(idx_ref[base + k], 1), :]
        here = mask_ref[pl.ds(unit * PER + j, 1), :]
        c = slice(j * BLOCK, (j + 1) * BLOCK)
        at = pl.ds(pl.multiple_of(base, BLOCK), BLOCK)
        blk = jnp.where(here > 0, g_ref[...].T, 0.0) + e_ref[:, at]
        if level < 2:
            lo, hi = blk[:BLOCK // 2], blk[BLOCK // 2:]
            first = idx_ref[F] == 0
            refs[0][:, c] = jnp.where(first, hi, lo)
            refs[1][:, c] = jnp.where(first, lo, hi)
        else:
            refs[0][:, c] = blk


def recv(level, half, idx, mask, y, entries):
    n, rows, outs = (2, BLOCK, 1) if level == 2 else (4, BLOCK // 2, 2)
    return pl.pallas_call(
        functools.partial(recv_kernel, level, n, half),
        grid=(n,),
        in_specs=[smem(), vmem(), vmem(), vmem()],
        out_specs=[pl.BlockSpec((rows, UNIT), lambda i: (0, i))] * outs,
        scratch_shapes=[pltpu.VMEM((BLOCK, BLOCK), F32)],
        out_shape=[jax.ShapeDtypeStruct((rows, n * UNIT), F32)] * outs,
        compiler_params=params(),
        cost_estimate=cost(0.9 * n),
        name="recv",
    )(idx, mask, y, entries)


def inv_small(D, n, step):
    rows = lax.broadcasted_iota(jnp.int32, (n, n), 0)
    cols = lax.broadcasted_iota(jnp.int32, (n, n), 1)
    lane = lax.broadcasted_iota(jnp.int32, (1, n), 1)
    for k in range(0, n, step):
        C = [jnp.broadcast_to(D[:, k + j:k + j + 1], (n, n)) for j in range(step)]
        B = [[C[j][k + i:k + i + 1, :] for j in range(step)] for i in range(step)]
        R = []
        for i in range(step):
            unit = jnp.where(lane == k + i, 1.0, 0.0)
            R.append(jnp.where((lane >= k) & (lane < k + step), unit, D[k + i:k + i + 1, :]))
        for p in range(step):
            d = 1.0 / B[p][p]
            for j in range(p + 1, step):
                B[p][j] = B[p][j] * d
            R[p] = R[p] * d
            for i in range(step):
                if i != p:
                    f = B[i][p]
                    for j in range(p + 1, step):
                        B[i][j] = B[i][j] - f * B[p][j]
                    R[i] = R[i] - f * R[p]
        D = jnp.where((cols >= k) & (cols < k + step), 0.0, D)
        for j in range(step):
            D = D - C[j] * R[j]
        for i in range(step):
            D = jnp.where(rows == k + i, R[i], D)
    return D


def inv_kernel(nb, a_ref, o_ref):
    o_ref[...] = a_ref[...].reshape(NP, NP)
    for b in range(NP // nb):
        lo = b * nb
        Ab = o_ref[:, lo:lo + nb]
        Dinv = inv_small(Ab[lo:lo + nb, :], nb, 8)
        lane = lax.broadcasted_iota(jnp.int32, (nb, NP), 1)
        eye = (lane - lo == lax.broadcasted_iota(jnp.int32, (nb, NP), 0)).astype(F32)
        Rb = jnp.where((lane >= lo) & (lane < lo + nb), eye, o_ref[lo:lo + nb, :])
        Rn = dot(Dinv, Rb)
        lane2 = lax.broadcasted_iota(jnp.int32, (NP, NP), 1)
        rest = jnp.where((lane2 >= lo) & (lane2 < lo + nb), 0.0, o_ref[...])
        o_ref[...] = rest - dot(Ab, Rn)
        o_ref[lo:lo + nb, :] = Rn


def inverse(got, first=0):
    last = got.shape[1] // PIV - 1
    return pl.pallas_call(
        functools.partial(inv_kernel, 64),
        grid=(1,),
        out_shape=jax.ShapeDtypeStruct((NP, NP), F32),
        in_specs=[pl.BlockSpec((NF, PIV, NP), lambda i: (0, last, first // NP))],
        out_specs=pl.BlockSpec((NP, NP), lambda i: (0, 0)),
        compiler_params=params(),
        cost_estimate=cost(12),
        name="inverse",
    )(got)


def last_kernel(a_ref, a12_ref, p_ref, inv_ref, m0_ref, m1_ref, mult_ref, top_ref):
    m = dot(p_ref[...], inv_ref[...])
    mult_ref[0] = m0_ref[PIV:, :]
    mult_ref[1] = m1_ref[PIV:, :]
    mult_ref[2] = m[PIV:, :]
    a12 = a12_ref[:, :, :UNIT].reshape(NP, UNIT)
    s = a_ref[...] - dot(m, a12)
    for j in range(PER):
        top_ref[:, j * UPD:(j + 1) * UPD] = s[PIV:, j * BLOCK + PIV:(j + 1) * BLOCK]


def last(a, a12, p, inv, m0, m1):
    return pl.pallas_call(
        last_kernel,
        out_shape=[jax.ShapeDtypeStruct((3, UPD, NP), F32), jax.ShapeDtypeStruct((UPD, PER * UPD), F32)],
        in_specs=[vmem()] * 6,
        out_specs=[vmem(), vmem()],
        compiler_params=params(),
        cost_estimate=cost(2),
        name="last",
    )(a, a12, p, inv, m0, m1)


def swap(x, axis, d):
    n = lax.axis_size(axis)
    return lax.ppermute(x, axis, [(i, i ^ d) for i in range(n)])


def part_of(x, i, size, dim):
    return lax.dynamic_slice_in_dim(x, i * size, size, dim)


def ordered(bit, mine, other):
    return jnp.where(bit == 0, mine, other), jnp.where(bit == 0, other, mine)


def tie(x, y):
    return lax.optimization_barrier((x, y))


def both_halves(x):
    both = jnp.stack(ordered(lax.axis_index("zh"), x, swap(x, "zh", 1)))
    return jnp.broadcast_to(both[None], (NF // 2,) + both.shape)


def gather_xy(out):
    got = lax.all_to_all(out, ("x", "y"), split_axis=0, concat_axis=0, tiled=True)
    return got.reshape((NF,) + out.shape[2:])


def shards(child_update, entries, slots):
    zl = lax.axis_index("zl")
    core = lax.axis_index("core")
    z0, z1 = zl & 1, zl >> 1
    front = lax.axis_index("x") * 8 + lax.axis_index("y") * 2 + lax.axis_index("zh")
    leaf = zl * 2 + core
    bits = [(core, "core", 1), (z0, "zl", 1), (z1, "zl", 2)]
    parts = [None, 64, 32]
    splits = [None, core, core * 2 + z0]

    plans = []
    for t in range(3):
        slot = lax.dynamic_index_in_dim(slots[t], (leaf >> t) << t, 0, keepdims=False)
        present = slot >= 0
        at = jnp.maximum(slot, 0)
        plan = {}
        if t == 0:
            col, row, mine = at, at, present
        else:
            blk, pos = at // UPD, at % UPD + PIV
            part, r = parts[t], splits[t]
            col = blk * BLOCK + pos
            mine = present & (pos // part == r)
            row = jnp.where(mine, blk * part + pos - part * r, 0)
            far = jnp.where(mine, blk * (part + PIV) + pos - part * r, 0)
            plan["sel"] = part_of(far, front, BLOCK, 0)
            plan["sel_mask"] = part_of(mine, front, BLOCK, 0).astype(F32)[:, None]
        plan["col"] = col
        plan["col_mask"] = present.astype(F32).reshape(NF, BLOCK)
        plan["row"] = jnp.concatenate([row, jnp.stack([core, z0] + [jnp.zeros_like(core)] * 126)])
        plan["row_mask"] = mine.astype(F32).reshape(NF, BLOCK)
        ep = entries[t, 0].reshape(BLOCK, NF, BLOCK)[:, :, :PIV].reshape(BLOCK, NP)
        plan["entries"] = entries[t, 0]
        piv_mask = plan["row_mask"][:, :PIV].reshape(1, NP)
        plan["ep"] = jnp.concatenate([ep, jnp.broadcast_to(piv_mask, (PIV, NP))])
        plans.append(plan)
    def placed(t, half, y):
        return recv(t, half, plans[t]["row"], plans[t]["row_mask"], y, plans[t]["entries"])

    def summed(x, steps):
        for bit, axis, d in steps:
            x = x + swap(x, axis, d)
        return x

    def exchange(out):
        return lax.all_to_all(out, FRONT, split_axis=0, concat_axis=0, tiled=True).reshape(-1, BLOCK)

    y = exchange(send(plans[0]["col"], plans[0]["col_mask"], (child_update[0],)))
    y, plans = tie(y, plans)
    p = panel(plans[0]["row"], y, plans[0]["ep"])
    p = summed(p, bits[:1])
    out = both_halves(jnp.concatenate([part_of(p, core, 64, 0), p[:PIV]], 0))
    y, out = tie(y, out)
    got0 = gather_xy(out)
    src = []
    for h in range(2):
        away, keep = placed(0, h, y)
        src.append((keep, swap(away, "core", 1)))
    out, got0 = tie(send(plans[1]["col"], plans[1]["col_mask"], *src), got0)

    y = exchange(out)
    inv0 = inverse(got0)
    m0 = dot(p, inv0)
    sel = jnp.take(got0.reshape(-1, NP), plans[1]["sel"], axis=0) * plans[1]["sel_mask"]
    child = (got0, summed(sel, bits[:1]), inv0)
    p = panel(plans[1]["row"], y, plans[1]["ep"], 64, (got0.reshape(-1, NP),) + child[1:])
    p = summed(p, bits[:1])
    y = correct(64, y, *child)
    y, p = tie(y, p)
    p = summed(p, bits[1:2])
    away, keep = placed(1, 0, y)
    p, away, keep = lax.optimization_barrier((p, away, keep))
    out = both_halves(jnp.concatenate([part_of(p, splits[2], 32, 0), p[:PIV]], 0))
    out, second = tie(out, placed(1, 1, y))
    got1 = gather_xy(out)
    src = []
    for away, keep in ((away, keep), second):
        rows = keep + swap(away, "core", 1)
        src.append((part_of(rows, z0, 32, 0), swap(part_of(rows, 1 - z0, 32, 0), "zl", 1)))
    out, got1 = tie(send(plans[2]["col"], plans[2]["col_mask"], *src), got1)

    y = exchange(out)
    inv1 = inverse(got1)
    m1 = dot(p, inv1)
    sel = jnp.take(got1.reshape(-1, NP), plans[2]["sel"], axis=0) * plans[2]["sel_mask"]
    child = (got1, summed(sel, bits[:2]), inv1)
    p = panel(plans[2]["row"], y, plans[2]["ep"], 32, (got1.reshape(-1, NP),) + child[1:])
    y = correct(32, y, *child)
    away = placed(2, (1, 1), y)[0]
    p, away = tie(summed(p, bits[:1]), away)
    far = placed(2, (1, 0), y)[0]
    p, far = tie(summed(p, bits[1:2]), far)
    moved = swap(far + swap(away, "core", 1), "zl", 1)
    away = placed(2, (0, 1), y)[0]
    near = placed(2, (0, 0), y)[0]
    p, near = tie(summed(p, bits[2:]), near)
    A = near + swap(away, "core", 1) + moved
    w = A.shape[1] // 2
    rows = A[:PIV]
    rows = part_of(rows, z1, w, 1) + swap(part_of(rows, 1 - z1, w, 1), "zl", 2)
    out = both_halves(jnp.concatenate([rows, p[:PIV]], 1))
    A, out = tie(A, out)
    got = gather_xy(out)
    inv2 = inverse(got, w)
    A = part_of(A, z1, w, 1) + swap(part_of(A, 1 - z1, w, 1), "zl", 2)
    A, inv2 = tie(A, inv2)
    mult, top = last(A, got, p, inv2, m0, m1)
    return mult[None], top


def solution(mesh):
    fine = Mesh(mesh.devices.reshape(4, 2, 4, 4, 2), LEAF + FRONT)
    in_specs = (P(LEAF, FRONT, None), P(None, LEAF, FRONT, None), P())
    out_specs = (P(LEAF, None, FRONT, None), P(FRONT, LEAF))
    return jax.shard_map(shards, mesh=fine, in_specs=in_specs, out_specs=out_specs, check_vma=False)
```

```python
import functools

import jax
import jax.numpy as jnp
from jax import lax
from jax.experimental import pallas as pl
from jax.experimental.pallas import tpu as pltpu
from jax.sharding import Mesh, PartitionSpec as P

F32 = jnp.float32
HIGHEST = lax.Precision.HIGHEST
BLOCK = 128
PIV = 8
UPD = BLOCK - PIV
NF = 32
F = NF * BLOCK
NP = NF * PIV
PER = 4
UNIT = PER * BLOCK
VMEM_LIMIT = 20 << 20
LEAF = ("zl", "core")
FRONT = ("x", "y", "zh")


def vmem():
    return pl.BlockSpec(memory_space=pltpu.VMEM)


def smem():
    return pl.BlockSpec(memory_space=pltpu.SMEM)


def params():
    return pltpu.CompilerParams(vmem_limit_bytes=VMEM_LIMIT)


def cost(us):
    return pl.CostEstimate(flops=0, bytes_accessed=int(us * 3.6e6), transcendentals=0)


def dot(a, b):
    return jnp.dot(a, b, precision=HIGHEST, preferred_element_type=F32)


def send_kernel(rows, pieces, terms, idx_ref, mask_ref, *refs):
    src, (out_ref, t_ref, g_ref) = refs[:-3], refs[-3:]
    step = pl.program_id(0)

    @pl.when(step == 0)
    def _():
        at = 0
        for p in range(pieces):
            for b in range(src[p * terms].shape[1] // BLOCK):
                blk = src[p * terms][:, b * BLOCK:(b + 1) * BLOCK]
                for j in range(1, terms):
                    blk = blk + src[p * terms + j][:, b * BLOCK:(b + 1) * BLOCK]
                if rows < BLOCK:
                    blk = jnp.concatenate([blk, jnp.zeros((BLOCK - rows, BLOCK), F32)], 0)
                t_ref[at:at + BLOCK, :] = blk.T
                at += BLOCK

    for j in range(PER):
        base = (step * PER + j) * BLOCK
        for k in range(BLOCK):
            g_ref[k:k + 1, :] = t_ref[pl.ds(idx_ref[base + k], 1), :]
        here = mask_ref[pl.ds(step * PER + j, 1), :]
        out_ref[j] = jnp.where(here > 0, g_ref[...].T[:rows], 0.0)


def send(idx, mask, *src):
    flat = [x for piece in src for x in piece]
    rows = flat[0].shape[0]
    cols = sum(piece[0].shape[1] for piece in src)
    return pl.pallas_call(
        functools.partial(send_kernel, rows, len(src), len(src[0])),
        grid=(NF // PER,),
        out_shape=jax.ShapeDtypeStruct((NF, rows, BLOCK), F32),
        in_specs=[smem()] + [vmem()] * (1 + len(flat)),
        out_specs=pl.BlockSpec((PER, rows, BLOCK), lambda i: (i, 0, 0)),
        scratch_shapes=[pltpu.VMEM((cols, BLOCK), F32), pltpu.VMEM((BLOCK, BLOCK), F32)],
        compiler_params=params(),
        cost_estimate=cost(7),
        name="send",
    )(idx, mask, *flat)


def place_pivots(idx_ref, pad, y_ref, g_ref):
    for k in range(NP):
        at = idx_ref[k // PIV * BLOCK + k % PIV]
        if pad:
            at = at + (at >> pad.bit_length() - 1) * PIV
        g_ref[k:k + 1, :] = y_ref[pl.ds(at, 1), :]


def store_pivots(rows, ep_ref, p_ref):
    for j in range(NP // BLOCK):
        c = slice(j * BLOCK, (j + 1) * BLOCK)
        p_ref[:, c] = jnp.where(ep_ref[BLOCK:BLOCK + 1, c] > 0, rows[c].T, 0.0) + ep_ref[:BLOCK, c]


def panel_kernel(idx_ref, y_ref, ep_ref, p_ref, g_ref):
    place_pivots(idx_ref, 0, y_ref, g_ref)
    store_pivots(g_ref[...], ep_ref, p_ref)


def panel_less_kernel(part, idx_ref, y_ref, ep_ref, got_ref, sel_ref, inv_ref, p_ref, g_ref, h_ref):
    place_pivots(idx_ref, 0, y_ref, g_ref)
    place_pivots(idx_ref, part, got_ref, h_ref)
    rows = g_ref[...] - dot(h_ref[...], dot(sel_ref[...], inv_ref[...]).T)
    store_pivots(rows, ep_ref, p_ref)


def panel(idx, y, ep, part=0, child=()):
    return pl.pallas_call(
        functools.partial(panel_less_kernel, part) if child else panel_kernel,
        out_shape=jax.ShapeDtypeStruct((BLOCK, NP), F32),
        in_specs=[smem()] + [vmem()] * (2 + len(child)),
        out_specs=vmem(),
        scratch_shapes=[pltpu.VMEM((NP, BLOCK), F32)] + [pltpu.VMEM((NP, NP), F32)] * (1 if child else 0),
        compiler_params=params(),
        cost_estimate=cost(3),
        name="panel",
    )(idx, y, ep, *child)


def correct_kernel(part, y_ref, got_ref, sel_ref, inv_ref, yc_ref, m_ref):
    @pl.when(pl.program_id(0) == 0)
    def _():
        m_ref[...] = dot(sel_ref[...], inv_ref[...]).T

    got = got_ref[:, :part, :].reshape(-1, NP)
    yc_ref[...] = y_ref[...] - dot(got, m_ref[...])


def correct(part, y, got, sel, inv):
    rows = y.shape[0] // 4
    return pl.pallas_call(
        functools.partial(correct_kernel, part),
        grid=(4,),
        out_shape=jax.ShapeDtypeStruct(y.shape, F32),
        in_specs=[
            pl.BlockSpec((rows, BLOCK), lambda i: (i, 0)),
            pl.BlockSpec((NF // 4, part + PIV, NP), lambda i: (i, 0, 0)),
            vmem(),
            vmem(),
        ],
        out_specs=pl.BlockSpec((rows, BLOCK), lambda i: (i, 0)),
        scratch_shapes=[pltpu.VMEM((NP, BLOCK), F32)],
        compiler_params=params(),
        cost_estimate=cost(4),
        name="correct",
    )(y, got, sel, inv)


def recv_kernel(level, n, half, idx_ref, mask_ref, y_ref, e_ref, *refs):
    g_ref = refs[-1]
    i = pl.program_id(0)
    if level < 2:
        unit = half * n + i
    else:
        z, c = half
        z = idx_ref[F + 1] if z == 0 else 1 - idx_ref[F + 1]
        c = idx_ref[F] if c == 0 else 1 - idx_ref[F]
        unit = i * 4 + z * 2 + c
    for j in range(PER):
        base = (unit * PER + j) * BLOCK
        for k in range(BLOCK):
            g_ref[k:k + 1, :] = y_ref[pl.ds(idx_ref[base + k], 1), :]
        here = mask_ref[pl.ds(unit * PER + j, 1), :]
        c = slice(j * BLOCK, (j + 1) * BLOCK)
        at = pl.ds(pl.multiple_of(base, BLOCK), BLOCK)
        blk = jnp.where(here > 0, g_ref[...].T, 0.0) + e_ref[:, at]
        if level < 2:
            lo, hi = blk[:BLOCK // 2], blk[BLOCK // 2:]
            first = idx_ref[F] == 0
            refs[0][:, c] = jnp.where(first, hi, lo)
            refs[1][:, c] = jnp.where(first, lo, hi)
        else:
            refs[0][:, c] = blk


def recv(level, half, idx, mask, y, entries):
    n, rows, outs = (2, BLOCK, 1) if level == 2 else (4, BLOCK // 2, 2)
    return pl.pallas_call(
        functools.partial(recv_kernel, level, n, half),
        grid=(n,),
        in_specs=[smem(), vmem(), vmem(), vmem()],
        out_specs=[pl.BlockSpec((rows, UNIT), lambda i: (0, i))] * outs,
        scratch_shapes=[pltpu.VMEM((BLOCK, BLOCK), F32)],
        out_shape=[jax.ShapeDtypeStruct((rows, n * UNIT), F32)] * outs,
        compiler_params=params(),
        cost_estimate=cost(0.9 * n),
        name="recv",
    )(idx, mask, y, entries)


def inv_small(D, n, step):
    rows = lax.broadcasted_iota(jnp.int32, (n, n), 0)
    cols = lax.broadcasted_iota(jnp.int32, (n, n), 1)
    lane = lax.broadcasted_iota(jnp.int32, (1, n), 1)
    for k in range(0, n, step):
        C = [jnp.broadcast_to(D[:, k + j:k + j + 1], (n, n)) for j in range(step)]
        B = [[C[j][k + i:k + i + 1, :] for j in range(step)] for i in range(step)]
        R = []
        for i in range(step):
            unit = jnp.where(lane == k + i, 1.0, 0.0)
            R.append(jnp.where((lane >= k) & (lane < k + step), unit, D[k + i:k + i + 1, :]))
        for p in range(step):
            d = 1.0 / B[p][p]
            for j in range(p + 1, step):
                B[p][j] = B[p][j] * d
            R[p] = R[p] * d
            for i in range(step):
                if i != p:
                    f = B[i][p]
                    for j in range(p + 1, step):
                        B[i][j] = B[i][j] - f * B[p][j]
                    R[i] = R[i] - f * R[p]
        D = jnp.where((cols >= k) & (cols < k + step), 0.0, D)
        for j in range(step):
            D = D - C[j] * R[j]
        for i in range(step):
            D = jnp.where(rows == k + i, R[i], D)
    return D


def inv_kernel(nb, a_ref, o_ref):
    o_ref[...] = a_ref[...].reshape(NP, NP)
    for b in range(NP // nb):
        lo = b * nb
        Ab = o_ref[:, lo:lo + nb]
        Dinv = inv_small(Ab[lo:lo + nb, :], nb, 8)
        lane = lax.broadcasted_iota(jnp.int32, (nb, NP), 1)
        eye = (lane - lo == lax.broadcasted_iota(jnp.int32, (nb, NP), 0)).astype(F32)
        Rb = jnp.where((lane >= lo) & (lane < lo + nb), eye, o_ref[lo:lo + nb, :])
        Rn = dot(Dinv, Rb)
        lane2 = lax.broadcasted_iota(jnp.int32, (NP, NP), 1)
        rest = jnp.where((lane2 >= lo) & (lane2 < lo + nb), 0.0, o_ref[...])
        o_ref[...] = rest - dot(Ab, Rn)
        o_ref[lo:lo + nb, :] = Rn


def inverse(got, first=0):
    last = got.shape[1] // PIV - 1
    return pl.pallas_call(
        functools.partial(inv_kernel, 64),
        grid=(1,),
        out_shape=jax.ShapeDtypeStruct((NP, NP), F32),
        in_specs=[pl.BlockSpec((NF, PIV, NP), lambda i: (0, last, first // NP))],
        out_specs=pl.BlockSpec((NP, NP), lambda i: (0, 0)),
        compiler_params=params(),
        cost_estimate=cost(12),
        name="inverse",
    )(got)


def last_kernel(a_ref, a12_ref, p_ref, inv_ref, m0_ref, m1_ref, mult_ref, top_ref):
    m = dot(p_ref[...], inv_ref[...])
    mult_ref[0] = m0_ref[PIV:, :]
    mult_ref[1] = m1_ref[PIV:, :]
    mult_ref[2] = m[PIV:, :]
    a12 = a12_ref[:, :, :UNIT].reshape(NP, UNIT)
    s = a_ref[...] - dot(m, a12)
    for j in range(PER):
        top_ref[:, j * UPD:(j + 1) * UPD] = s[PIV:, j * BLOCK + PIV:(j + 1) * BLOCK]


def last(a, a12, p, inv, m0, m1):
    return pl.pallas_call(
        last_kernel,
        out_shape=[jax.ShapeDtypeStruct((3, UPD, NP), F32), jax.ShapeDtypeStruct((UPD, PER * UPD), F32)],
        in_specs=[vmem()] * 6,
        out_specs=[vmem(), vmem()],
        compiler_params=params(),
        cost_estimate=cost(2),
        name="last",
    )(a, a12, p, inv, m0, m1)


def swap(x, axis, d):
    n = lax.axis_size(axis)
    return lax.ppermute(x, axis, [(i, i ^ d) for i in range(n)])


def part_of(x, i, size, dim):
    return lax.dynamic_slice_in_dim(x, i * size, size, dim)


def ordered(bit, mine, other):
    return jnp.where(bit == 0, mine, other), jnp.where(bit == 0, other, mine)


def tie(x, y):
    return lax.optimization_barrier((x, y))


def both_halves(x):
    both = jnp.stack(ordered(lax.axis_index("zh"), x, swap(x, "zh", 1)))
    return jnp.broadcast_to(both[None], (NF // 2,) + both.shape)


def gather_xy(out):
    got = lax.all_to_all(out, ("x", "y"), split_axis=0, concat_axis=0, tiled=True)
    return got.reshape((NF,) + out.shape[2:])


def shards(child_update, entries, slots):
    zl = lax.axis_index("zl")
    core = lax.axis_index("core")
    z0, z1 = zl & 1, zl >> 1
    front = lax.axis_index("x") * 8 + lax.axis_index("y") * 2 + lax.axis_index("zh")
    leaf = zl * 2 + core
    bits = [(core, "core", 1), (z0, "zl", 1), (z1, "zl", 2)]
    parts = [None, 64, 32]
    splits = [None, core, core * 2 + z0]

    plans = []
    for t in range(3):
        slot = lax.dynamic_index_in_dim(slots[t], (leaf >> t) << t, 0, keepdims=False)
        present = slot >= 0
        at = jnp.maximum(slot, 0)
        plan = {}
        if t == 0:
            col, row, mine = at, at, present
        else:
            blk, pos = at // UPD, at % UPD + PIV
            part, r = parts[t], splits[t]
            col = blk * BLOCK + pos
            mine = present & (pos // part == r)
            row = jnp.where(mine, blk * part + pos - part * r, 0)
            far = jnp.where(mine, blk * (part + PIV) + pos - part * r, 0)
            plan["sel"] = part_of(far, front, BLOCK, 0)
            plan["sel_mask"] = part_of(mine, front, BLOCK, 0).astype(F32)[:, None]
        plan["col"] = col
        plan["col_mask"] = present.astype(F32).reshape(NF, BLOCK)
        plan["row"] = jnp.concatenate([row, jnp.stack([core, z0] + [jnp.zeros_like(core)] * 126)])
        plan["row_mask"] = mine.astype(F32).reshape(NF, BLOCK)
        ep = entries[t, 0].reshape(BLOCK, NF, BLOCK)[:, :, :PIV].reshape(BLOCK, NP)
        plan["entries"] = entries[t, 0]
        piv_mask = plan["row_mask"][:, :PIV].reshape(1, NP)
        plan["ep"] = jnp.concatenate([ep, jnp.broadcast_to(piv_mask, (PIV, NP))])
        plans.append(plan)
    def placed(t, half, y):
        return recv(t, half, plans[t]["row"], plans[t]["row_mask"], y, plans[t]["entries"])

    def summed(x, steps):
        for bit, axis, d in steps:
            x = x + swap(x, axis, d)
        return x

    def exchange(out):
        return lax.all_to_all(out, FRONT, split_axis=0, concat_axis=0, tiled=True).reshape(-1, BLOCK)

    y = exchange(send(plans[0]["col"], plans[0]["col_mask"], (child_update[0],)))
    y, plans = tie(y, plans)
    p = panel(plans[0]["row"], y, plans[0]["ep"])
    p = summed(p, bits[:1])
    out = both_halves(jnp.concatenate([part_of(p, core, 64, 0), p[:PIV]], 0))
    y, out = tie(y, out)
    got0 = gather_xy(out)
    src = []
    for h in range(2):
        away, keep = placed(0, h, y)
        src.append((keep, swap(away, "core", 1)))
    out, got0 = tie(send(plans[1]["col"], plans[1]["col_mask"], *src), got0)

    y = exchange(out)
    inv0 = inverse(got0)
    m0 = dot(p, inv0)
    sel = jnp.take(got0.reshape(-1, NP), plans[1]["sel"], axis=0) * plans[1]["sel_mask"]
    child = (got0, summed(sel, bits[:1]), inv0)
    p = panel(plans[1]["row"], y, plans[1]["ep"], 64, (got0.reshape(-1, NP),) + child[1:])
    p = summed(p, bits[:1])
    y = correct(64, y, *child)
    y, p = tie(y, p)
    p = summed(p, bits[1:2])
    away, keep = placed(1, 0, y)
    p, away, keep = lax.optimization_barrier((p, away, keep))
    out = both_halves(jnp.concatenate([part_of(p, splits[2], 32, 0), p[:PIV]], 0))
    out, second = tie(out, placed(1, 1, y))
    got1 = gather_xy(out)
    src = []
    for away, keep in ((away, keep), second):
        rows = keep + swap(away, "core", 1)
        src.append((part_of(rows, z0, 32, 0), swap(part_of(rows, 1 - z0, 32, 0), "zl", 1)))
    out, got1 = tie(send(plans[2]["col"], plans[2]["col_mask"], *src), got1)

    y = exchange(out)
    inv1 = inverse(got1)
    m1 = dot(p, inv1)
    sel = jnp.take(got1.reshape(-1, NP), plans[2]["sel"], axis=0) * plans[2]["sel_mask"]
    child = (got1, summed(sel, bits[:2]), inv1)
    p = panel(plans[2]["row"], y, plans[2]["ep"], 32, (got1.reshape(-1, NP),) + child[1:])
    y = correct(32, y, *child)
    away = placed(2, (1, 1), y)[0]
    p, away = tie(summed(p, bits[:1]), away)
    far = placed(2, (1, 0), y)[0]
    p, far = tie(summed(p, bits[1:2]), far)
    moved = swap(far + swap(away, "core", 1), "zl", 1)
    away = placed(2, (0, 1), y)[0]
    near = placed(2, (0, 0), y)[0]
    p, near = tie(summed(p, bits[2:]), near)
    A = near + swap(away, "core", 1) + moved
    w = A.shape[1] // 2
    rows = A[:PIV]
    rows = part_of(rows, z1, w, 1) + swap(part_of(rows, 1 - z1, w, 1), "zl", 2)
    out = both_halves(jnp.concatenate([rows, p[:PIV]], 1))
    A, out = tie(A, out)
    got = gather_xy(out)
    inv2 = inverse(got, w)
    moved = swap(part_of(A, 1 - z1, w, 1), "zl", 2)
    A, inv2 = tie(part_of(A, z1, w, 1), inv2)
    A = A + moved
    mult, top = last(A, got, p, inv2, m0, m1)
    return mult[None], top


def solution(mesh):
    fine = Mesh(mesh.devices.reshape(4, 2, 4, 4, 2), LEAF + FRONT)
    in_specs = (P(LEAF, FRONT, None), P(None, LEAF, FRONT, None), P())
    out_specs = (P(LEAF, None, FRONT, None), P(FRONT, LEAF))
    return jax.shard_map(shards, mesh=fine, in_specs=in_specs, out_specs=out_specs, check_vma=False)
```
